256 devices in a mesh: gx: 64 (over x, z, core), gy: 2 (over y_lo), gz: 2 (over y_hi).
Axes of the slice: x: 4, y: 4 (y_hi: 2, y_lo: 2; y = y_hi * 2 + y_lo), z: 8, core: 2. Of those that a mesh axis runs over, the one named last changes fastest.
Arguments:
- fields: float32 [7, 2048, 64, 256], P(None, 'gx', 'gy', 'gz'), may hold values from -6 to 6
- retained: int32 [64, 2, 8, 7, 3], P('gx', 'gy', 'gz'), may hold values from 0 to 1, as said below
Outputs:
- stream: bfloat16 [2, 2, 460544, 128], P('gy', 'gz', 'gx')
The draws below stay inside these ranges and needn't reach their ends.
Inputs may be any that keep to these rules, and one draw needn't show every extreme that they name: `retained`: 1 where the block keeps that level's details of that field, 0 where it drops them.
All inputs are finite; a program needn't handle non-finite values.
Results may differ from the reference program's by a relative error of at most 0.001.
Values may be sent and summed in bfloat16 or wider, within the bound.
No kernel may reach another device: no remote copies, remote signals or barrier semaphores. Data moves between devices by JAX's collectives and lax.ppermute only.
A program may use at most 192 MiB of HBM per device.

```python
import jax
import jax.numpy as jnp
from jax import lax

FIELDS = 7
BLK = 32
LEVELS = 3
GROUP = 128
NBLK = 4
P1 = 224
P2 = 28
P3 = 4
P0 = 1
CAP = 7196
NX = 2048
NY = 64
NZ = 256
N_GX = 64
N_GY = 2
N_GZ = 2


def draw_retained(key, part):
    key = jax.random.fold_in(key, 11)
    rolls = jax.random.randint(key, (N_GX, N_GY, N_GZ * NBLK, FIELDS, LEVELS), 0, 1000)
    ramp = 250 + 600 * jnp.arange(N_GX, dtype=jnp.int32) // (N_GX - 1)
    return (rolls < ramp[:, None, None, None, None]).astype(jnp.int32)


def shard_levels(stream_key, dims, cuts, low, high):
    factor_of = 1.0
    for axis_at, parts in cuts:
        steps = jax.random.uniform(jax.random.fold_in(jax.random.fold_in(stream_key, 6), axis_at), (parts,), jnp.float32, low / len(cuts), high / len(cuts))
        factor_of = factor_of * jnp.repeat(jnp.exp(steps), dims[axis_at] // parts).reshape((-1,) + (1,) * (len(dims) - 1 - axis_at))
    return factor_of


def centred(stream_key, shape, deviation, limit, cuts=(), kind=jnp.bfloat16):
    entries = jax.random.normal(stream_key, shape, jnp.float32) * deviation
    if len(cuts) > 0:
        entries = shard_levels(stream_key, shape, cuts, -0.22, 0.18) * entries
    return jnp.clip(entries, min=-limit, max=limit).astype(kind)


def setup_inputs(seed: int = 0) -> dict:
    splits = jax.random.split(jax.random.key(seed), 3)
    return {
        "fields": centred(splits[0], (FIELDS, NX, NY, NZ), 1.0, 6.0, ((1, 64), (2, 2), (3, 2)), jnp.float32),
        "retained": draw_retained(jax.random.fold_in(splits[2], 71), 0),
    }


def lift_axis(lattice, axis_position_index):
    extent = lattice.shape[axis_position_index]
    even_samples = lax.slice_in_dim(lattice, 0, extent, 2, axis_position_index)
    odd_samples = lax.slice_in_dim(lattice, 1, extent, 2, axis_position_index)
    predicted_values = (9.0 / 16.0) * (even_samples + jnp.roll(even_samples, -1, axis_position_index)) - (1.0 / 16.0) * (jnp.roll(even_samples, 1, axis_position_index) + jnp.roll(even_samples, -2, axis_position_index))
    return even_samples, odd_samples - predicted_values


def one_level(lattice):
    subbands = [lattice]
    for axis_position_index in range(3):
        lifted = []
        for entry in subbands:
            lifted.extend(lift_axis(entry, axis_position_index))
        subbands = lifted
    return subbands[0], jnp.stack(subbands[1:])


def block_packets(values, block_edge, groups):
    band_count = values.shape[0]
    shaped = values.reshape(band_count, N_GX, block_edge, N_GY, block_edge, N_GZ, NBLK, block_edge)
    shaped = shaped.transpose(1, 3, 5, 6, 0, 2, 4, 7)
    shaped = shaped.reshape(N_GX, N_GY, N_GZ, NBLK, band_count * block_edge ** 3)
    padded = jnp.pad(shaped, ((0, 0), (0, 0), (0, 0), (0, 0), (0, groups * GROUP - band_count * block_edge ** 3)))
    return padded.reshape(N_GX, N_GY, N_GZ, NBLK, groups, GROUP).astype(jnp.bfloat16)


def field_layout(field):
    lattice = field
    pieces = []
    for level_index, groups in ((1, P1), (2, P2), (3, P3)):
        lattice, details = one_level(lattice)
        pieces.append(block_packets(details, BLK // 2 ** level_index, groups))
    pieces.append(block_packets(lattice[None], BLK // 8, P0))
    return jnp.concatenate(pieces[::-1], axis=4)


def row_compact(pair):
    values, live_flag = pair
    position = (jnp.cumsum(live_flag) - 1).astype(jnp.int32)
    target = jnp.where(live_flag > 0, position, live_flag.shape[0])
    return jnp.zeros_like(values).at[target].set(values, mode="drop")


def reference(fields, retained):
    layout = lax.map(field_layout, fields)
    layout = layout.transpose(2, 3, 1, 0, 4, 5, 6).reshape(N_GY * N_GZ, N_GX * CAP, GROUP)
    flags = retained.reshape(N_GX, N_GY, N_GZ, NBLK, FIELDS, LEVELS).transpose(1, 2, 0, 4, 3, 5)
    always = jnp.ones_like(flags[..., :1])
    flag_parts = [always, flags[..., 2:3], flags[..., 1:2], flags[..., 0:1]]
    group_spans = [P0, P3, P2, P1]
    live_flag = jnp.concatenate([jnp.broadcast_to(flag_part, flag_part.shape[:-1] + (group_span,)) for flag_part, group_span in zip(flag_parts, group_spans)], axis=-1)
    live_flag = live_flag.reshape(N_GY * N_GZ, N_GX * CAP).astype(jnp.int32)
    stream = lax.map(row_compact, (layout, live_flag))
    return stream.reshape(N_GY, N_GZ, N_GX * CAP, GROUP)
```

```python
import functools

import jax
import jax.numpy as jnp
from jax import lax
from jax.experimental import pallas as pl
from jax.experimental.pallas import tpu as pltpu
from jax.sharding import PartitionSpec as P

P1 = 224
P2 = 28
P3 = 4
P0 = 1
CAP = 7196
NF = 7
NB = 4
F32 = jnp.float32
BF16 = jnp.bfloat16
W9 = 9.0 / 16.0
W1 = 1.0 / 16.0

HALO = (0, 2, 4, 8, 24, 28, 30)
PAIR = (0, 2, 30, 4, 28, 0, 2, 30)


def lanes(rows):
    return lax.broadcasted_iota(jnp.int32, (rows, 128), 1)


def subs(rows):
    return lax.broadcasted_iota(jnp.int32, (rows, 128), 0)


def pick(values, index):
    return jnp.take_along_axis(values, index, axis=1)


def table(which, entries):
    out = jnp.full(which.shape, entries[0], type(entries[0]) is float and F32 or jnp.int32)
    for k, entry in enumerate(entries):
        if k > 0:
            out = jnp.where(which == k, entry, out)
    return out


def pack_kernel(f_ref, xh, xl, yy, zz, xyh, xyl, xz, yz, xyz):
    col = lanes(32) % 8
    ia = table(col, (0, 0, 0, 0, 126, 124, 120, 0))
    ib = table(col, (2, 4, 8, 0, 0, 0, 0, 0))
    ca = table(col, (W9, W9, W9, -W1, -W1, -W1, -W1, 0.0))
    cb = table(col, (-W1, -W1, -W1, 0.0, 0.0, 0.0, 0.0, 0.0))
    chunk = lanes(32) // 8

    def ends(x):
        v = f_ref[0, x]
        return ca * pick(v, ia) + cb * pick(v, ib)

    for half in range(2):
        acc = jnp.zeros((32, 128), F32)
        for k in range(16):
            acc = jnp.where(chunk == k, ends(half * 16 + k), acc)
        zz[0, half] = acc
        for j, row in enumerate(PAIR):
            yz[0, half, j] = acc[row]
        for j in range(8):
            yz[0, 2 + half, j] = acc[8 if j % 2 == 0 else 24]
    acc = jnp.zeros((32, 128), F32)
    for k, x in enumerate(HALO):
        acc = jnp.where(chunk == k, ends(x), acc)
    xz[0] = acc
    for j, row in enumerate(HALO + (30,)):
        xyz[0, j] = acc[row]
    for k, x in enumerate(HALO):
        plane, corner, k = (xh, xyh, k) if k < 4 else (xl, xyl, k - 4)
        plane[0, k] = f_ref[0, x]
        for j, row in enumerate(HALO + (30,)):
            corner[0, k, j] = f_ref[0, x, row]
    for k in range(16):
        for j, row in enumerate(PAIR):
            yy[0, k, j] = f_ref[0, 2 * k + (j >= 5), row]
    for k in range(8):
        for j in range(2):
            yy[0, 16 + k // 4, (k % 4) * 2 + j] = f_ref[0, 4 * k, (8, 24)[j]]


def field_block(*shape):
    return pl.BlockSpec((1,) + shape, lambda f: (f,) + (0,) * len(shape))


HALO_SHAPES = (
    (4, 32, 128),
    (3, 32, 128),
    (18, 8, 128),
    (2, 32, 128),
    (4, 8, 128),
    (3, 8, 128),
    (32, 128),
    (4, 8, 128),
    (8, 128),
)


def pack(fields):
    return pl.pallas_call(
        pack_kernel,
        grid=(NF,),
        in_specs=[field_block(32, 32, 128)],
        out_specs=[field_block(*shape) for shape in HALO_SHAPES],
        out_shape=[jax.ShapeDtypeStruct((NF,) + shape, F32) for shape in HALO_SHAPES],
        name="pack",
    )(fields)


def lift_lanes(v, ends, step):
    lane = lanes(v.shape[0])
    odd = lane % (2 * step) == step
    c9l = jnp.where(odd, W9, 0.0)
    c9r = jnp.where(odd & (lane != 128 - step), W9, 0.0)
    c1l = jnp.where(odd & (lane != step), W1, 0.0)
    c1r = jnp.where(odd & (lane != 128 - step) & (lane != 128 - 3 * step), W1, 0.0)
    edge = (lane == step) | (lane == 128 - step) | (lane == 128 - 3 * step)
    near = c9l * pltpu.roll(v, step, 1) + c9r * pltpu.roll(v, 128 - step, 1)
    far = c1l * pltpu.roll(v, 3 * step, 1) + c1r * pltpu.roll(v, 128 - 3 * step, 1)
    return v - ((near - far) + jnp.where(edge, ends, 0.0))


def end_index(rows, step):
    lane = lanes(rows)
    level = {1: 0, 2: 1, 4: 2}[step]
    return jnp.where(
        lane == step, 4 + level, jnp.where(lane == 128 - step, level, 3)
    )


def predicted(a, b, c, d):
    return W9 * (b + c) - W1 * (a + d)


def shuffle_indices(level):
    lane, sub = lanes(8), subs(8)
    r = (lane // 16 - sub) % 8
    w = lane % 16
    b, hz = r // 2, r % 2
    if level == 1:
        first = b * 32 + w * 2 + hz
        y, rest = lane // 16, lane % 16
    elif level == 2:
        first = b * 32 + (w % 8) * 4 + hz * 2 + w // 8
        y, rest = (lane // 8) % 8, (lane // 64) * 8 + lane % 8
    else:
        first = b * 32 + (w % 4) * 8 + hz * 4 + w // 4
        y = (lane // 64) * 4 + (lane // 4) % 4
        rest = ((lane // 16) % 4) * 4 + lane % 4
    last = ((y + sub) % 8) * 16 + rest
    return first, r, last


def shuffle(tile, indices):
    first, middle, last = indices
    tile = jnp.take_along_axis(tile, first, axis=1)
    tile = jnp.take_along_axis(tile, middle, axis=0)
    return jnp.take_along_axis(tile, last, axis=1)


def main_kernel(
    me, cnt, ret, f_ref, xh, xl, yy, zz, xyh, xyl, xzh, xzl, yz, xyzh, xyzl,
    out, z1, z2, z3, st1, st2, st3, t3, ring, pos,
):
    field = pl.program_id(0)
    nblk, rows = out.shape[0], out.shape[1]

    @pl.when(field == 0)
    def _():
        total = lax.fori_loop(0, me[0], lambda i, s: s + cnt[i], jnp.int32(0))
        pos[0] = total % CAP
        pos[1] = total % CAP

    levels = ((1, z1, 32), (2, z2, 16), (4, z3, 8))

    for step, z, n in levels:
        index = end_index(n, step)

        def plane(j, _, step=step, z=z, n=n, index=index):
            x = j * step
            if step == 1:
                v, e = f_ref[0, x], zz[0, x // 16]
            else:
                v = f_ref[0, x, pl.ds(0, n, stride=step), :]
                e = zz[0, x // 16, pl.ds(0, n, stride=step), :]
            z[j + 2, pl.ds(8, n)] = lift_lanes(v, pick(e, index + (x % 16) * 8), step)
            return _

        lax.fori_loop(0, n, plane, 0, unroll=2)

    second = subs(8) >= 5

    def pair(k, _):
        v, e = yy[0, k], yz[0, k // 8]
        base = jnp.where(second, ((2 * k + 1) % 16) * 8, ((2 * k) % 16) * 8)
        r = lift_lanes(v, pick(e, base + end_index(8, 1)), 1)
        for half in range(2):
            p = 2 * k + 2 + half
            z1[p, 40] = r[5 * half]
            z1[p, 42] = r[5 * half + 1]
            z1[p, 6] = r[5 * half + 2]
        r = lift_lanes(v, pick(e, base + end_index(8, 2)), 2)
        z2[k + 2, 24] = r[0]
        z2[k + 2, 26] = r[3]
        z2[k + 2, 6] = r[4]
        return _

    lax.fori_loop(0, 16, pair, 0, unroll=2)
    for k in range(8):
        r = lift_lanes(yy[0, 2 * k], pick(yz[0, k // 4], (4 * k % 16) * 8 + end_index(8, 4)), 4)
        z3[k + 2, 16] = r[0]
    for half in range(2):
        base = (subs(8) // 2) * 32
        r = lift_lanes(yy[0, 16 + half], pick(yz[0, 2 + half], base + end_index(8, 4)), 4)
        for k in range(4):
            z3[half * 4 + k + 2, 18] = r[2 * k]
            z3[half * 4 + k + 2, 6] = r[2 * k + 1]

    for lev, (step, z, n) in enumerate(levels):
        for p, at in ((0, n + 2), (1 + lev, n + 4), (6 - lev, 0)):
            if p < 4:
                planes, ends, corner, cends, q = xh, xzh, xyh, xyzh, p
            else:
                planes, ends, corner, cends, q = xl, xzl, xyl, xyzl, p - 4
            if step == 1:
                v, e = planes[0, q], ends[0]
            else:
                v = planes[0, q, pl.ds(0, n, stride=step), :]
                e = ends[0, pl.ds(0, n, stride=step), :]
            z[at, pl.ds(8, n)] = lift_lanes(v, pick(e, p * 8 + end_index(n, step)), step)
            r = lift_lanes(corner[0, q], pick(cends[0], p * 8 + end_index(8, step)), step)
            z[at, 8 + n] = r[0]
            z[at, 10 + n] = r[1 + lev]
            z[at, 6] = r[6 - lev]

    def lifted_rows(z, p, n):
        def rows_from(start):
            return z[p, pl.ds(start, n // 2, stride=2), :]

        low = rows_from(8)
        return low, rows_from(9) - predicted(rows_from(6), low, rows_from(10), rows_from(12))

    def lift_plane(z, p):
        z[p] = z[p] - predicted(z[p - 3], z[p - 1], z[p + 1], z[p + 3])

    shuffle1 = shuffle_indices(1)

    def pair1(k, _):
        lift_plane(z1, 2 * k + 3)
        for hx in range(2):
            for hy, side in enumerate(lifted_rows(z1, 2 * k + 2 + hx, 32)):
                for top in range(2):
                    tile = shuffle(side[8 * top : 8 * top + 8], shuffle1)
                    start = (2 * hx + hy) * 256 + 2 * k + top
                    st1[pl.ds(start, 8, stride=32), :] = tile
        return _

    lax.fori_loop(0, 16, pair1, 0)

    shuffle2 = shuffle_indices(2)
    even_lane = lanes(8) % 2 == 0

    def pair2(q, _):
        for hx in range(2):
            both = []
            for xlo in range(2):
                k = 2 * q + xlo
                if hx == 1:
                    lift_plane(z2, 2 * k + 3)
                both.append(lifted_rows(z2, 2 * k + 2 + hx, 16))
            for hy in range(2):
                tile = jnp.where(even_lane, both[0][hy], pltpu.roll(both[1][hy], 1, 1))
                tile = shuffle(tile, shuffle2)
                for r in range(8):
                    b, hz = r // 2, r % 2
                    st2[b * 32 + (4 * hx + 2 * hy + hz) * 4 + q] = tile[r]
        return _

    lax.fori_loop(0, 4, pair2, 0)

    shuffle3 = shuffle_indices(3)
    lane8 = lanes(8)
    tiles = []
    for hx in range(2):
        acc = [None, None]
        for k in range(4):
            if hx == 1:
                lift_plane(z3, 2 * k + 3)
            for hy, side in enumerate(lifted_rows(z3, 2 * k + 2 + hx, 8)):
                if k == 0:
                    acc[hy] = side
                else:
                    acc[hy] = jnp.where(lanes(4) % 4 == k, pltpu.roll(side, k, 1), acc[hy])
        t3[pl.ds(0, 4)] = acc[0]
        t3[pl.ds(4, 4)] = acc[1]
        tiles.append(shuffle(t3[...], shuffle3))
    left = lane8 < 64
    a, c = tiles
    ar, cr = pltpu.roll(a, 64, 1), pltpu.roll(c, 64, 1)

    def above(t):
        return pltpu.roll(t, 1, 0)

    groups = (
        jnp.where(left, above(a), 0.0),
        jnp.where(left, a, above(a)),
        jnp.where(left, ar, above(cr)),
        jnp.where(left, c, above(c)),
        jnp.where(left, cr, 0.0),
    )
    for b in range(NB):
        for j, group in enumerate(groups):
            st3[b * 8 + j] = group[2 * b + 1]

    for b in range(NB):
        flags = [ret[(b * NF + field) * 3 + lev] for lev in range(3)]
        here = pos[0]
        ring[pl.ds(here, 8)] = st3[pl.ds(b * 8, 8)]
        at2 = here + P0 + P3 * flags[2]
        at1 = at2 + P2 * flags[1]
        pos[0] = at1 + P1 * flags[0]

        @pl.when(flags[1] > 0)
        def _(b=b, at2=at2):
            ring[pl.ds(at2, 32)] = st2[pl.ds(b * 32 + 4, 32)]

        @pl.when(flags[0] > 0)
        def _(b=b, at1=at1):
            for s in range(1, 8):
                start = ((s // 2) * 8 + b * 2 + s % 2) * 32
                ring[pl.ds(at1 + (s - 1) * 32, 32)] = st1[pl.ds(start, 32)]

    @pl.when(field == NF - 1)
    def _():
        first = pos[1]
        used = -(-CAP // rows)
        tile = 128 if rows % 128 == 0 else 16

        def fold(i, _):
            at = i * tile
            slot = at + subs(tile)
            near = ring[pl.ds(pl.multiple_of(at, 8), tile)]
            far = ring[pl.ds(at + CAP, tile)]
            value = jnp.where(slot >= first, near, far).astype(BF16)
            out[at // rows, pl.ds(pl.multiple_of(at % rows, 16), tile)] = value
            return _

        lax.fori_loop(0, used * rows // tile, fold, 0)
        for block in range(used, nblk):
            out[block] = jnp.zeros((rows, 128), BF16)


def smem():
    return pl.BlockSpec(memory_space=pltpu.SMEM)


def transform(me, counts, flags, fields, halos, blocks, rows):
    shapes = ((32, 32, 128),) + tuple(h.shape[1:] for h in halos)
    ring_rows = 2 * CAP + rows + 128
    return pl.pallas_call(
        main_kernel,
        grid=(NF,),
        in_specs=[smem(), smem(), smem()] + [field_block(*shape) for shape in shapes],
        out_specs=pl.BlockSpec((blocks, rows, 128), lambda f: (0, 0, 0)),
        out_shape=jax.ShapeDtypeStruct((blocks, rows, 128), BF16),
        scratch_shapes=[
            pltpu.VMEM((37, 48, 128), F32),
            pltpu.VMEM((21, 32, 128), F32),
            pltpu.VMEM((13, 24, 128), F32),
            pltpu.VMEM((1024, 128), F32),
            pltpu.VMEM((168, 128), F32),
            pltpu.VMEM((32, 128), F32),
            pltpu.VMEM((8, 128), F32),
            pltpu.VMEM((ring_rows, 128), F32),
            pltpu.SMEM((2,), jnp.int32),
        ],
        compiler_params=pltpu.CompilerParams(vmem_limit_bytes=40 * 2**20),
        name="transform",
    )(me, counts, flags, fields, *halos)


def route_kernel(me, cnt, recv, send):
    n, rows = recv.shape[0], recv.shape[1]
    slot = me[0] * rows + subs(rows)
    send[...] = jnp.zeros_like(send)

    def one(i, begin):
        count = cnt[i]
        place, first = begin // CAP, begin % CAP
        end = first + count
        value = recv[i]
        here = (slot >= first) & (slot < jnp.minimum(end, CAP))
        send[place] = jnp.where(here, value, send[place])

        @pl.when(end > CAP)
        def _():
            send[place + 1] = jnp.where(slot < end - CAP, value, send[place + 1])

        return begin + count

    lax.fori_loop(0, n, one, jnp.int32(0))


def route(me, counts, received):
    return pl.pallas_call(
        route_kernel,
        in_specs=[smem(), smem(), pl.BlockSpec(memory_space=pltpu.VMEM)],
        out_specs=pl.BlockSpec(memory_space=pltpu.VMEM),
        out_shape=jax.ShapeDtypeStruct(received.shape, BF16),
        compiler_params=pltpu.CompilerParams(vmem_limit_bytes=40 * 2**20),
        name="route",
    )(me, counts, received)


def neighbour(value, n, dx, dy, dz):
    pairs = []
    for x in range(n):
        for y in range(2):
            for z in range(2):
                source = (((x + dx) % n) * 2 + (y + dy) % 2) * 2 + (z + dz) % 2
                pairs.append((source, (x * 2 + y) * 2 + z))
    return lax.ppermute(value, ("gx", "gy", "gz"), pairs)


def per_device(n, fields, retained):
    me = lax.axis_index("gx").astype(jnp.int32).reshape(1)
    flags = retained.reshape(NB * NF, 3)
    live = NB * NF * P0 + jnp.sum(flags * jnp.array([[P1, P2, P3]], jnp.int32))
    counts = lax.all_gather(live.reshape(1), "gx", tiled=True)
    xh, xl, yy, zz, xyh, xyl, xz, yz, xyz = pack(fields)
    move = functools.partial(neighbour, n=n)
    halos = (
        move(xh, dx=1, dy=0, dz=0),
        move(xl, dx=-1, dy=0, dz=0),
        move(yy, dx=0, dy=1, dz=0),
        move(zz, dx=0, dy=0, dz=1),
        move(xyh, dx=1, dy=1, dz=0),
        move(xyl, dx=-1, dy=1, dz=0),
        move(xz, dx=1, dy=0, dz=1),
        move(xz, dx=-1, dy=0, dz=1),
        move(yz, dx=0, dy=1, dz=1),
        move(xyz, dx=1, dy=1, dz=1),
        move(xyz, dx=-1, dy=1, dz=1),
    )
    rows = -(-CAP // (16 * n)) * 16
    ring = transform(me, counts, flags.reshape(-1), fields, halos, n, rows)
    spread = lax.all_to_all(ring, "gx", 0, 0, tiled=True)
    routed = route(me, counts, spread)
    stream = lax.all_to_all(routed, "gx", 0, 0, tiled=True)
    return stream.reshape(1, 1, n * rows, 128)[:, :, :CAP]


def solution(mesh):
    placed = (P(None, "gx", "gy", "gz"), P("gx", "gy", "gz", None, None))
    return jax.shard_map(
        functools.partial(per_device, mesh.shape["gx"]),
        mesh=mesh,
        in_specs=placed,
        out_specs=P("gy", "gz", "gx", None),
        check_vma=False,
    )
```

```python
import functools

import jax
import jax.numpy as jnp
from jax import lax
from jax.experimental import pallas as pl
from jax.experimental.pallas import tpu as pltpu
from jax.sharding import PartitionSpec as P

P1 = 224
P2 = 28
P3 = 4
P0 = 1
CAP = 7196
NF = 7
NB = 4
F32 = jnp.float32
BF16 = jnp.bfloat16
W9 = 9.0 / 16.0
W1 = 1.0 / 16.0

LEVEL_ROWS = ((0, 2, 30), (0, 4, 28), (0, 8, 24))
PAIR = (0, 2, 30, 4, 28, 0, 2, 30)
CORNERS = (
    tuple((0, row) for row in (0, 2, 4, 8, 24, 28, 30, 30)),
    tuple((1, row) for row in (0, 2, 30)) + tuple((6, row) for row in (0, 2, 30, 30, 30)),
    tuple((2, row) for row in (0, 4, 28)) + tuple((5, row) for row in (0, 4, 28, 28, 28)),
    tuple((3, row) for row in (0, 8, 24)) + tuple((4, row) for row in (0, 8, 24, 24, 24)),
)
TILES = 22


def lanes(rows, width=128):
    return lax.broadcasted_iota(jnp.int32, (rows, width), 1)


def subs(rows, width=128):
    return lax.broadcasted_iota(jnp.int32, (rows, width), 0)


def thirds(v):
    high = v.astype(BF16)
    rest = v - high.astype(F32)
    mid = rest.astype(BF16)
    low = (rest - mid.astype(F32)).astype(BF16)
    return jnp.concatenate([high, mid, low], axis=1)


def dot(a, b):
    return jnp.dot(a, b, preferred_element_type=F32)


def field_block(*shape):
    return pl.BlockSpec((1,) + shape, lambda f, *_: (f,) + (0,) * len(shape))


def smem():
    return pl.BlockSpec(memory_space=pltpu.SMEM)


def planes_kernel(odd, a, b, core, other):
    core[...] = a[...]
    other[...] = b[...]


def boundary_planes(odd, fields):
    def plane(k, high):
        return jnp.where(high, (1 << k) & 14, 32 - (8 >> k))

    block = (NF, 1, 32, 128)
    shape = jax.ShapeDtypeStruct((NF, 4, 32, 128), F32)
    return pl.pallas_call(
        planes_kernel,
        grid_spec=pltpu.PrefetchScalarGridSpec(
            num_scalar_prefetch=1,
            grid=(4,),
            in_specs=[
                pl.BlockSpec(block, lambda k, odd: (0, plane(k, odd[0] == 1), 0, 0)),
                pl.BlockSpec(block, lambda k, odd: (0, plane(k, odd[0] == 0), 0, 0)),
            ],
            out_specs=[pl.BlockSpec(block, lambda k, odd: (0, k, 0, 0))] * 2,
        ),
        out_shape=[shape, shape],
        name="planes",
    )(odd, fields, fields)


def halo_plane(odd, core, other, p):
    if p < 4:
        return jnp.where(odd == 1, other[0, p], core[0, p])
    return jnp.where(odd == 1, core[0, p - 4], other[0, p - 4])


END_A = (0, 0, 0, 0, 124, 126, 120, 0)
END_B = (4, 0, 8, 2, 0, 0, 0, 0)


def pack_kernel(odd_ref, f_ref, core, other, yy, zz, yz, ends):
    odd = odd_ref[0]

    @pl.when(pl.program_id(0) == 0)
    def _():
        lane, row = lanes(384) % 8, subs(384) % 128
        weight = jnp.zeros((384, 128), F32)
        for col in range(7):
            joint = col in (0, 2, 3)
            weight = jnp.where((lane == col) & (row == END_A[col]), W9 if joint else -W1, weight)
            if joint:
                weight = jnp.where((lane == col) & (row == END_B[col]), -W1, weight)
        ends[...] = weight.astype(BF16)

    chunk = lanes(32) // 8
    weight = ends[...]
    for part in range(3):
        if part < 2:
            planes = [f_ref[0, part * 16 + k] for k in range(16)]
        else:
            planes = [halo_plane(odd, core, other, p) for p in range(7)]
        made = dot(thirds(jnp.concatenate(planes, axis=0)), weight)
        acc = jnp.zeros((32, 128), F32)
        for k in range(len(planes)):
            acc = jnp.where(chunk == k, made[32 * k : 32 * k + 32], acc)
        zz[0, part] = acc

    for half in range(2):
        for j, row in enumerate(PAIR):
            yz[0, half, j] = zz[0, half, row]
        for j in range(8):
            yz[0, 2 + half, j] = zz[0, half, 8 if j % 2 == 0 else 24]
    for t, corner in enumerate(CORNERS):
        for j, (_, row) in enumerate(corner):
            yz[0, 4 + t, j] = zz[0, 2, row]

    for k in range(16):
        for j, row in enumerate(PAIR):
            yy[0, k, j] = f_ref[0, 2 * k + (j >= 5), row]
    for k in range(8):
        for j in range(2):
            yy[0, 16 + k // 4, (k % 4) * 2 + j] = f_ref[0, 4 * k, (8, 24)[j]]
    whole = [halo_plane(odd, core, other, p) for p in range(7)]
    for t, corner in enumerate(CORNERS):
        for j, (p, row) in enumerate(corner):
            yy[0, 18 + t, j] = whole[p][row]


def pack(odd, fields, core, other):
    shapes = ((TILES, 8, 128), (3, 32, 128), (8, 8, 128))
    return pl.pallas_call(
        pack_kernel,
        grid=(NF,),
        in_specs=[smem(), field_block(32, 32, 128)] + [field_block(4, 32, 128)] * 2,
        out_specs=[field_block(*shape) for shape in shapes],
        out_shape=[jax.ShapeDtypeStruct((NF,) + shape, F32) for shape in shapes],
        scratch_shapes=[pltpu.VMEM((384, 128), BF16)],
        compiler_params=pltpu.CompilerParams(vmem_limit_bytes=40 * 2**20),
        name="pack",
    )(odd, fields, core, other)


STEPS = (1, 2, 4)


def lift_matrix(step):
    row, lane = subs(384) % 128, lanes(384)
    odd = lane % (2 * step) == step
    apart = jnp.abs(row - lane)
    weight = jnp.where(odd & (apart == step), -W9, 0.0)
    weight = jnp.where(odd & (apart == 3 * step), W1, weight)
    return jnp.where(apart == 0, 1.0, weight).astype(BF16)


def at_ends(ends, step):
    lane = lanes(ends.shape[0])
    edge = (lane == step) | (lane == 128 - step) | (lane == 128 - 3 * step)
    return jnp.where(edge, ends, 0.0)


def end_index(rows):
    lane = lanes(rows)
    index = jnp.ones_like(lane)
    for at, col in ((126, 0), (124, 2), (127, 3), (2, 4), (1, 5), (4, 6)):
        index = jnp.where(lane == at, col, index)
    return index


def predicted(a, b, c, d):
    return W9 * (b + c) - W1 * (a + d)


def pick(values, index):
    return jnp.take_along_axis(values, index, axis=1)


def packet_matrix(level, y):
    lane, col = subs(128, 1024), lanes(128, 1024)
    r, at = col // 128, col % 128
    b, hz = r // 2, r % 2
    if level == 1:
        source, row = b * 32 + (at % 16) * 2 + hz, at // 16
    else:
        source = b * 32 + (at % 8) * 4 + hz * 2 + at // 64
        row = (at // 8) % 8
    return jnp.where((lane == source) & (row == y), 1.0, 0.0).astype(BF16)


def shuffle_indices():
    lane, sub = lanes(8), subs(8)
    r = (lane // 16 - sub) % 8
    w = lane % 16
    first = (r // 2) * 32 + (w % 4) * 8 + (r % 2) * 4 + w // 4
    y = (lane // 64) * 4 + (lane // 4) % 4
    rest = ((lane // 16) % 4) * 4 + lane % 4
    return first, r, ((y + sub) % 8) * 16 + rest


def shuffle(tile, indices):
    first, middle, last = indices
    tile = jnp.take_along_axis(tile, first, axis=1)
    tile = jnp.take_along_axis(tile, middle, axis=0)
    return jnp.take_along_axis(tile, last, axis=1)


def main_kernel(
    me, cnt, ret, f_ref, core, other, yy, zz, yz,
    out, z1, z2, z3, in2, out2, st1, st3, t3, ring, lifts, sort1, sort2,
):
    field = pl.program_id(0)
    nblk, rows = out.shape[0], out.shape[1]
    odd = me[0] % 2

    @pl.when(field == 0)
    def _():
        for lev, step in enumerate(STEPS):
            lifts[:, lev * 128 : lev * 128 + 128] = lift_matrix(step)
        for y in range(8):
            sort1[y * 128 : y * 128 + 128] = packet_matrix(1, y)
            sort2[y * 128 : y * 128 + 128] = packet_matrix(2, y)

    def planes1(g, _):
        weight = lifts[:, 0:128]
        made = dot(thirds(f_ref[0, pl.ds(8 * g, 8)].reshape(256, 128)), weight)
        for k in range(8):
            x = 8 * g + k
            e = pltpu.roll(zz[0, x // 16], (124 - 8 * (x % 16)) % 128, 1)
            to = pl.multiple_of((x + 2) * 48 + 8, 8)
            z1[pl.ds(to, 32)] = made[32 * k : 32 * k + 32] - at_ends(e, 1)
        return _

    lax.fori_loop(0, 4, planes1, 0)

    def cells(lev, x):
        step = STEPS[lev]
        return f_ref[0, x, pl.ds(0, 32 // step, stride=step), :]

    def ends_of(lev, part, k):
        step = STEPS[lev]
        n = 32 // step
        e = zz[0, part, pl.ds(0, n, stride=step), :] if step > 1 else zz[0, part]
        return at_ends(pick(e, end_index(n) + 8 * k), step)

    for lev, z, to in ((1, z2, lambda j: j * 32 + 8), (2, z3, lambda j: j * 24 + 8)):
        step = STEPS[lev]
        n = 32 // step
        v = jnp.concatenate([cells(lev, j * step) for j in range(n)], axis=0)
        made = dot(thirds(v), lifts[:, lev * 128 : lev * 128 + 128])
        for j in range(n):
            x = j * step
            z[pl.ds(to(j + 2), n)] = made[n * j : n * j + n] - ends_of(lev, x // 16, x % 16)

    sides = [halo_plane(odd, core, other, p) for p in range(7)]
    for lev, (z, pitch) in enumerate(((z1, 48), (z2, 32), (z3, 24))):
        step = STEPS[lev]
        n = 32 // step
        which = ((0, n + 2), (1 + lev, n + 4), (6 - lev, 0))
        for p, at in which:
            t3[pl.ds(0, 32)] = sides[p]
            v = t3[pl.ds(0, n, stride=step), :] if step > 1 else sides[p]
            made = dot(thirds(v), lifts[:, lev * 128 : lev * 128 + 128])
            z[pl.ds(at * pitch + 8, n)] = made - ends_of(lev, 2, p)

    made = dot(thirds(yy[0].reshape(TILES * 8, 128)), lifts[...])
    sub, index = subs(8), end_index(8)
    ends = []
    for t in range(TILES):
        if t < 16:
            e, chunk = yz[0, t // 8], jnp.where(sub < 5, 2 * t % 16, (2 * t + 1) % 16)
        elif t < 18:
            e, chunk = yz[0, 2 + t - 16], (sub // 2) * 4
        elif t == 18:
            e, chunk = yz[0, 4], 0
        else:
            e, chunk = yz[0, t - 14], jnp.where(sub < 3, t - 18, 25 - t)
        ends.append(pick(e, index + 8 * chunk))
    ends = jnp.concatenate(ends, axis=0)
    for lev, (z, pitch) in enumerate(((z1, 48), (z2, 32), (z3, 24))):
        step = STEPS[lev]
        n = 32 // step
        r = made[:, lev * 128 : lev * 128 + 128] - at_ends(ends, step)

        def put(j, first, second, last, z=z, pitch=pitch, n=n, r=r):
            for at, row in ((8 + n, first), (10 + n, second), (6, last)):
                z[pl.ds(j * pitch + at, 1)] = r[row : row + 1]

        for j in range(n):
            if lev == 0:
                at = (j // 2) * 8 + 5 * (j % 2)
                put(j + 2, at, at + 1, at + 2)
            elif lev == 1:
                put(j + 2, j * 8, j * 8 + 3, j * 8 + 4)
            else:
                put(j + 2, j * 16, 128 + 2 * j, 129 + 2 * j)
        put(n + 2, 18 * 8, 18 * 8 + 1 + lev, 18 * 8 + 6 - lev)
        at = (19 + lev) * 8
        put(n + 4, at, at + 1, at + 2)
        put(0, at + 3, at + 4, at + 5)

    def lift_plane(z, pitch, p):
        def plane(q):
            return z[pl.ds(pl.multiple_of(q * pitch, 8), pitch)]

        z[pl.ds(pl.multiple_of(p * pitch, 8), pitch)] = plane(p) - predicted(
            plane(p - 3), plane(p - 1), plane(p + 1), plane(p + 3)
        )

    def lift1(k, _):
        lift_plane(z1, 48, 2 * k + 3)
        return _

    lax.fori_loop(0, 16, lift1, 0, unroll=2)
    for k in range(8):
        lift_plane(z2, 32, 2 * k + 3)
    for k in range(4):
        lift_plane(z3, 24, 2 * k + 3)

    def lifted(load, count):
        low = [load(2 * j) for j in range(-1, count + 2)]
        high = [
            load(2 * j + 1) - predicted(low[j], low[j + 1], low[j + 2], low[j + 3])
            for j in range(count)
        ]
        return low[1 : count + 1], high

    parts = []
    for hx in range(2):
        sides = lifted(
            lambda y: z1[pl.ds((2 + hx) * 48 + 8 + y, 16, stride=96), :], 16
        )
        for side in sides:
            for top in range(2):
                tiles = [v.astype(BF16) for v in side[8 * top : 8 * top + 8]]
                parts.append(jnp.concatenate(tiles, axis=1))
    made = dot(jnp.concatenate(parts, axis=0), sort1[...])
    for c in range(8):
        for r in range(8):
            at = field * 1024 + ((c // 2) * 8 + r) * 32 + c % 2
            st1[pl.ds(at, 16, stride=2), :] = made[16 * c : 16 * c + 16, 128 * r : 128 * r + 128]

    even_lane = lanes(8) % 2 == 0
    parts = []
    for hx in range(2):
        sides = lifted(
            lambda y: z2[pl.ds((2 + hx) * 32 + 8 + y, 8, stride=64), :], 8
        )
        for side in sides:
            tiles = []
            for v in side:
                after = pltpu.roll(pltpu.roll(v, 7, 0), 1, 1)
                tiles.append(jnp.where(even_lane, v, after))
            parts.append(jnp.concatenate(tiles, axis=1))
    in2[pl.ds(pl.multiple_of(field * 32, 32), 32)] = jnp.concatenate(parts, axis=0).astype(BF16)

    lane8 = lanes(8)
    tiles = []
    for hx in range(2):
        acc = [None, None]
        for k in range(4):
            base = (2 * k + 2 + hx) * 24

            def rows_from(start, base=base):
                return z3[pl.ds(base + start, 4, stride=2), :]

            low = rows_from(8)
            high = rows_from(9) - predicted(rows_from(6), low, rows_from(10), rows_from(12))
            for hy, side in enumerate((low, high)):
                if k == 0:
                    acc[hy] = side
                else:
                    acc[hy] = jnp.where(lanes(4) % 4 == k, pltpu.roll(side, k, 1), acc[hy])
        t3[pl.ds(0, 4)] = acc[0]
        t3[pl.ds(4, 4)] = acc[1]
        tiles.append(shuffle(t3[pl.ds(0, 8)], shuffle_indices()))
    left = lane8 < 64
    a, c = tiles
    ar, cr = pltpu.roll(a, 64, 1), pltpu.roll(c, 64, 1)

    def above(t):
        return pltpu.roll(t, 1, 0)

    groups = (
        jnp.where(left, above(a), 0.0),
        jnp.where(left, a, above(a)),
        jnp.where(left, ar, above(cr)),
        jnp.where(left, c, above(c)),
        jnp.where(left, cr, 0.0),
    )
    for b in range(NB):
        for j, group in enumerate(groups):
            st3[pl.ds(field * 32 + b * 8 + j, 1)] = group[2 * b + 1 : 2 * b + 2]

    @pl.when(field == NF - 1)
    def _():
        made = dot(in2[...], sort2[...])
        for r in range(8):
            out2[r] = made[:, 128 * r : 128 * r + 128]
        total = lax.fori_loop(0, me[0], lambda i, s: s + cnt[i], jnp.int32(0))
        first = total % CAP

        def one(f, here):
            for b in range(NB):
                flags = [ret[(b * NF + f) * 3 + lev] for lev in range(3)]
                ring[pl.ds(here, 8)] = st3[pl.ds(pl.multiple_of(f * 32 + b * 8, 8), 8)]
                at2 = here + P0 + P3 * flags[2]
                at1 = at2 + P2 * flags[1]
                here = at1 + P1 * flags[0]

                @pl.when(flags[1] > 0)
                def _(b=b, at2=at2):
                    for s in range(1, 8):
                        r = b * 2 + s % 2
                        ring[pl.ds(at2 + (s - 1) * 4, 4)] = out2[
                            r, pl.ds(f * 32 + (s // 2) * 8, 4, stride=2), :
                        ]

                @pl.when(flags[0] > 0)
                def _(b=b, at1=at1):
                    for s in range(1, 8):
                        start = f * 1024 + ((s // 2) * 8 + b * 2 + s % 2) * 32
                        ring[pl.ds(at1 + (s - 1) * 32, 32)] = st1[
                            pl.ds(pl.multiple_of(start, 32), 32)
                        ]
            return here

        lax.fori_loop(0, NF, one, first)
        used = -(-CAP // rows)

        def fold(i, _):
            at = pl.multiple_of(i * rows, 8)
            near, far = ring[pl.ds(at, rows)], ring[pl.ds(at + CAP, rows)]
            out[i] = jnp.where(at + subs(rows) >= first, near, far).astype(BF16)
            return _

        lax.fori_loop(0, used, fold, 0)
        for block in range(used, nblk):
            out[block] = jnp.zeros((rows, 128), BF16)


def transform(me, counts, flags, fields, halos, blocks, rows):
    shapes = ((32, 32, 128),) + tuple(h.shape[1:] for h in halos)
    ring_rows = (2 * CAP + rows + 135) // 8 * 8
    return pl.pallas_call(
        main_kernel,
        grid=(NF,),
        in_specs=[smem(), smem(), smem()] + [field_block(*shape) for shape in shapes],
        out_specs=pl.BlockSpec((blocks, rows, 128), lambda f: (0, 0, 0)),
        out_shape=jax.ShapeDtypeStruct((blocks, rows, 128), BF16),
        scratch_shapes=[
            pltpu.VMEM((37 * 48, 128), F32),
            pltpu.VMEM((21 * 32, 128), F32),
            pltpu.VMEM((13 * 24, 128), F32),
            pltpu.VMEM((NF * 32, 1024), BF16),
            pltpu.VMEM((8, NF * 32, 128), F32),
            pltpu.VMEM((NF * 1024, 128), F32),
            pltpu.VMEM((NF * 32, 128), F32),
            pltpu.VMEM((32, 128), F32),
            pltpu.VMEM((ring_rows, 128), F32),
            pltpu.VMEM((384, 384), BF16),
            pltpu.VMEM((1024, 1024), BF16),
            pltpu.VMEM((1024, 1024), BF16),
        ],
        compiler_params=pltpu.CompilerParams(vmem_limit_bytes=48 * 2**20),
        name="transform",
    )(me, counts, flags, fields, *halos)


def route_kernel(me, cnt, recv, send):
    n, rows = recv.shape[0], recv.shape[1]
    slot = me[0] * rows + subs(rows)
    send[...] = jnp.zeros_like(send)

    def one(i, begin):
        count = cnt[i]
        place, first = begin // CAP, begin % CAP
        end = first + count
        value = recv[i]
        here = (slot >= first) & (slot < jnp.minimum(end, CAP))
        send[place] = jnp.where(here, value, send[place])

        @pl.when(end > CAP)
        def _():
            send[place + 1] = jnp.where(slot < end - CAP, value, send[place + 1])

        return begin + count

    lax.fori_loop(0, n, one, jnp.int32(0))


def route(me, counts, received):
    return pl.pallas_call(
        route_kernel,
        in_specs=[smem(), smem(), pl.BlockSpec(memory_space=pltpu.VMEM)],
        out_specs=pl.BlockSpec(memory_space=pltpu.VMEM),
        out_shape=jax.ShapeDtypeStruct(received.shape, BF16),
        compiler_params=pltpu.CompilerParams(vmem_limit_bytes=40 * 2**20),
        name="route",
    )(me, counts, received)


def swapped(value, n, axis, dy=0, dz=0):
    pairs = []
    for x in range(n):
        to = (x, x ^ 1, (x + 1 if x % 2 else x - 1) % n)[axis]
        for y in range(2):
            for z in range(2):
                there = (to * 2 + (y + dy) % 2) * 2 + (z + dz) % 2
                pairs.append(((x * 2 + y) * 2 + z, there))
    return lax.ppermute(value, ("gx", "gy", "gz"), pairs)


def per_device(n, fields, retained):
    me = lax.axis_index("gx").astype(jnp.int32).reshape(1)
    odd = me % 2
    flags = retained.reshape(NB * NF, 3)
    live = NB * NF * P0 + jnp.sum(flags * jnp.array([[P1, P2, P3]], jnp.int32))
    core, other = boundary_planes(odd, fields)
    core, other = swapped(core, n, 1), swapped(other, n, 2)
    yy, zz, yz = pack(odd, fields, core, other)
    counts = lax.all_gather(live.reshape(1), "gx", tiled=True)
    halos = (
        core,
        other,
        swapped(yy, n, 0, dy=1),
        swapped(zz, n, 0, dz=1),
        swapped(yz, n, 0, dy=1, dz=1),
    )
    rows = -(-CAP // (8 * n)) * 8
    ring = transform(me, counts, flags.reshape(-1), fields, halos, n, rows)
    spread = lax.all_to_all(ring, "gx", 0, 0, tiled=True)
    routed = route(me, counts, spread)
    stream = lax.all_to_all(routed, "gx", 0, 0, tiled=True)
    return stream.reshape(1, 1, n * rows, 128)[:, :, :CAP]


def solution(mesh):
    placed = (P(None, "gx", "gy", "gz"), P("gx", "gy", "gz", None, None))
    return jax.shard_map(
        functools.partial(per_device, mesh.shape["gx"]),
        mesh=mesh,
        in_specs=placed,
        out_specs=P("gy", "gz", "gx", None),
        check_vma=False,
    )
```

```python
import functools

import jax
import jax.numpy as jnp
from jax import lax
from jax.experimental import pallas as pl
from jax.experimental.pallas import tpu as pltpu
from jax.sharding import PartitionSpec as P

P1 = 224
P2 = 28
P3 = 4
P0 = 1
CAP = 7196
NF = 7
NB = 4
F32 = jnp.float32
BF16 = jnp.bfloat16
W9 = 9.0 / 16.0
W1 = 1.0 / 16.0

LEVEL_ROWS = ((0, 2, 30), (0, 4, 28), (0, 8, 24))
PAIR = (0, 2, 30, 4, 28, 0, 2, 30)
CORNERS = (
    tuple((0, row) for row in (0, 2, 4, 8, 24, 28, 30, 30)),
    tuple((1, row) for row in (0, 2, 30)) + tuple((6, row) for row in (0, 2, 30, 30, 30)),
    tuple((2, row) for row in (0, 4, 28)) + tuple((5, row) for row in (0, 4, 28, 28, 28)),
    tuple((3, row) for row in (0, 8, 24)) + tuple((4, row) for row in (0, 8, 24, 24, 24)),
)
TILES = 22


def lanes(rows, width=128):
    return lax.broadcasted_iota(jnp.int32, (rows, width), 1)


def subs(rows, width=128):
    return lax.broadcasted_iota(jnp.int32, (rows, width), 0)


def thirds(v):
    high = v.astype(BF16)
    rest = v - high.astype(F32)
    mid = rest.astype(BF16)
    low = (rest - mid.astype(F32)).astype(BF16)
    return jnp.concatenate([high, mid, low], axis=1)


def dot(a, b):
    return jnp.dot(a, b, preferred_element_type=F32)


def field_block(*shape):
    return pl.BlockSpec((1,) + shape, lambda f, *_: (f,) + (0,) * len(shape))


def smem():
    return pl.BlockSpec(memory_space=pltpu.SMEM)


def planes_kernel(odd, *refs):
    core, other = refs[8:]
    for k in range(4):
        core[:, k] = refs[2 * k][:, 0]
        other[:, k] = refs[2 * k + 1][:, 0]


def boundary_planes(odd, fields):
    def block(k, j):
        high, low = (1 << k) & 14, 32 - (8 >> k)
        return pl.BlockSpec(
            (NF, 1, 32, 128),
            lambda i, odd: (0, jnp.where(odd[0] == 1 - j, high, low), 0, 0),
        )

    shape = (NF, 4, 32, 128)
    return pl.pallas_call(
        planes_kernel,
        grid_spec=pltpu.PrefetchScalarGridSpec(
            num_scalar_prefetch=1,
            grid=(1,),
            in_specs=[block(k, j) for k in range(4) for j in range(2)],
            out_specs=[pl.BlockSpec(shape, lambda i, odd: (0, 0, 0, 0))] * 2,
        ),
        out_shape=[jax.ShapeDtypeStruct(shape, F32)] * 2,
        name="planes",
    )(odd, *[fields] * 8)


def halo_plane(odd, core, other, p):
    if p < 4:
        return jnp.where(odd == 1, other[0, p], core[0, p])
    return jnp.where(odd == 1, core[0, p - 4], other[0, p - 4])


END_A = (0, 0, 0, 0, 124, 126, 120, 0)
END_B = (4, 0, 8, 2, 0, 0, 0, 0)


def pack_kernel(me, ret, f_ref, core, other, yy, zz, yz, count, ends):
    odd = me[0] % 2

    @pl.when(pl.program_id(0) == 0)
    def _():
        live = jnp.int32(NB * NF * P0)
        for i in range(NB * NF):
            live = live + ret[3 * i] * P1 + ret[3 * i + 1] * P2 + ret[3 * i + 2] * P3
        for i in range(count.shape[0]):
            count[i] = jnp.where(me[0] == i, live, 0)
        lane, row = lanes(384) % 8, subs(384) % 128
        weight = jnp.zeros((384, 128), F32)
        for col in range(7):
            joint = col in (0, 2, 3)
            weight = jnp.where((lane == col) & (row == END_A[col]), W9 if joint else -W1, weight)
            if joint:
                weight = jnp.where((lane == col) & (row == END_B[col]), -W1, weight)
        ends[...] = weight.astype(BF16)

    chunk = lanes(32) // 8
    weight = ends[...]
    for part in range(3):
        if part < 2:
            planes = [f_ref[0, part * 16 + k] for k in range(16)]
        else:
            planes = [halo_plane(odd, core, other, p) for p in range(7)]
        made = dot(thirds(jnp.concatenate(planes, axis=0)), weight)
        acc = jnp.zeros((32, 128), F32)
        for k in range(len(planes)):
            acc = jnp.where(chunk == k, made[32 * k : 32 * k + 32], acc)
        zz[0, part] = acc

    for half in range(2):
        for j, row in enumerate(PAIR):
            yz[0, half, j] = zz[0, half, row]
        for j in range(8):
            yz[0, 2 + half, j] = zz[0, half, 8 if j % 2 == 0 else 24]
    for t, corner in enumerate(CORNERS):
        for j, (_, row) in enumerate(corner):
            yz[0, 4 + t, j] = zz[0, 2, row]

    for k in range(16):
        for j, row in enumerate(PAIR):
            yy[0, k, j] = f_ref[0, 2 * k + (j >= 5), row]
    for k in range(8):
        for j in range(2):
            yy[0, 16 + k // 4, (k % 4) * 2 + j] = f_ref[0, 4 * k, (8, 24)[j]]
    whole = [halo_plane(odd, core, other, p) for p in range(7)]
    for t, corner in enumerate(CORNERS):
        for j, (p, row) in enumerate(corner):
            yy[0, 18 + t, j] = whole[p][row]


def pack(me, flags, fields, core, other, n):
    shapes = ((TILES, 8, 128), (3, 32, 128), (8, 8, 128))
    return pl.pallas_call(
        pack_kernel,
        grid=(NF,),
        in_specs=[smem(), smem(), field_block(32, 32, 128)] + [field_block(4, 32, 128)] * 2,
        out_specs=[field_block(*shape) for shape in shapes] + [smem()],
        out_shape=[jax.ShapeDtypeStruct((NF,) + shape, F32) for shape in shapes]
        + [jax.ShapeDtypeStruct((n,), jnp.int32)],
        scratch_shapes=[pltpu.VMEM((384, 128), BF16)],
        compiler_params=pltpu.CompilerParams(vmem_limit_bytes=40 * 2**20),
        name="pack",
    )(me, flags, fields, core, other)


STEPS = (1, 2, 4)


def lift_matrix(step):
    row, lane = subs(384) % 128, lanes(384)
    odd = lane % (2 * step) == step
    apart = jnp.abs(row - lane)
    weight = jnp.where(odd & (apart == step), -W9, 0.0)
    weight = jnp.where(odd & (apart == 3 * step), W1, weight)
    return jnp.where(apart == 0, 1.0, weight).astype(BF16)


def at_ends(ends, step):
    lane = lanes(ends.shape[0])
    edge = (lane == step) | (lane == 128 - step) | (lane == 128 - 3 * step)
    return jnp.where(edge, ends, 0.0)


def end_index(rows):
    lane = lanes(rows)
    index = jnp.ones_like(lane)
    for at, col in ((126, 0), (124, 2), (127, 3), (2, 4), (1, 5), (4, 6)):
        index = jnp.where(lane == at, col, index)
    return index


def predicted(a, b, c, d):
    return W9 * (b + c) - W1 * (a + d)


def pick(values, index):
    return jnp.take_along_axis(values, index, axis=1)


def packet_matrix(level, y):
    lane, col = subs(128, 1024), lanes(128, 1024)
    r, at = col // 128, col % 128
    b, hz = r // 2, r % 2
    if level == 1:
        source, row = b * 32 + (at % 16) * 2 + hz, at // 16
    else:
        source = b * 32 + (at % 8) * 4 + hz * 2 + at // 64
        row = (at // 8) % 8
    return jnp.where((lane == source) & (row == y), 1.0, 0.0).astype(BF16)


def shuffle_indices():
    lane, sub = lanes(8), subs(8)
    r = (lane // 16 - sub) % 8
    w = lane % 16
    first = (r // 2) * 32 + (w % 4) * 8 + (r % 2) * 4 + w // 4
    y = (lane // 64) * 4 + (lane // 4) % 4
    rest = ((lane // 16) % 4) * 4 + lane % 4
    return first, r, ((y + sub) % 8) * 16 + rest


def shuffle(tile, indices):
    first, middle, last = indices
    tile = jnp.take_along_axis(tile, first, axis=1)
    tile = jnp.take_along_axis(tile, middle, axis=0)
    return jnp.take_along_axis(tile, last, axis=1)


def main_kernel(
    me, cnt, ret, f_ref, core, other, yy, zz, yz,
    out, z1, z2, z3, in2, out2, st1, st3, t3, ring, lifts, sort1, sort2,
):
    field = pl.program_id(0)
    nblk, rows = out.shape[0], out.shape[1]
    odd = me[0] % 2

    @pl.when(field == 0)
    def _():
        for lev, step in enumerate(STEPS):
            lifts[:, lev * 128 : lev * 128 + 128] = lift_matrix(step)
        for y in range(8):
            sort1[y * 128 : y * 128 + 128] = packet_matrix(1, y)
            sort2[y * 128 : y * 128 + 128] = packet_matrix(2, y)

    weight = lifts[:, 0:128]
    for g in range(4):
        made = dot(thirds(f_ref[0, 8 * g : 8 * g + 8].reshape(256, 128)), weight)
        for k in range(8):
            x = 8 * g + k
            e = pltpu.roll(zz[0, x // 16], (124 - 8 * (x % 16)) % 128, 1)
            z1[pl.ds((x + 2) * 48 + 8, 32)] = made[32 * k : 32 * k + 32] - at_ends(e, 1)

    def cells(lev, x):
        step = STEPS[lev]
        return f_ref[0, x, pl.ds(0, 32 // step, stride=step), :]

    def ends_of(lev, part, k):
        step = STEPS[lev]
        n = 32 // step
        e = zz[0, part, pl.ds(0, n, stride=step), :] if step > 1 else zz[0, part]
        return at_ends(pick(e, end_index(n) + 8 * k), step)

    for lev, z, to in ((1, z2, lambda j: j * 32 + 8), (2, z3, lambda j: j * 24 + 8)):
        step = STEPS[lev]
        n = 32 // step
        v = jnp.concatenate([cells(lev, j * step) for j in range(n)], axis=0)
        made = dot(thirds(v), lifts[:, lev * 128 : lev * 128 + 128])
        for j in range(n):
            x = j * step
            z[pl.ds(to(j + 2), n)] = made[n * j : n * j + n] - ends_of(lev, x // 16, x % 16)

    sides = [halo_plane(odd, core, other, p) for p in range(7)]
    for lev, (z, pitch) in enumerate(((z1, 48), (z2, 32), (z3, 24))):
        step = STEPS[lev]
        n = 32 // step
        which = ((0, n + 2), (1 + lev, n + 4), (6 - lev, 0))
        for p, at in which:
            t3[pl.ds(0, 32)] = sides[p]
            v = t3[pl.ds(0, n, stride=step), :] if step > 1 else sides[p]
            made = dot(thirds(v), lifts[:, lev * 128 : lev * 128 + 128])
            z[pl.ds(at * pitch + 8, n)] = made - ends_of(lev, 2, p)

    made = dot(thirds(yy[0].reshape(TILES * 8, 128)), lifts[...])
    sub, index = subs(8), end_index(8)
    ends = []
    for t in range(TILES):
        if t < 16:
            e, chunk = yz[0, t // 8], jnp.where(sub < 5, 2 * t % 16, (2 * t + 1) % 16)
        elif t < 18:
            e, chunk = yz[0, 2 + t - 16], (sub // 2) * 4
        elif t == 18:
            e, chunk = yz[0, 4], 0
        else:
            e, chunk = yz[0, t - 14], jnp.where(sub < 3, t - 18, 25 - t)
        ends.append(pick(e, index + 8 * chunk))
    ends = jnp.concatenate(ends, axis=0)
    for lev, (z, pitch) in enumerate(((z1, 48), (z2, 32), (z3, 24))):
        step = STEPS[lev]
        n = 32 // step
        r = made[:, lev * 128 : lev * 128 + 128] - at_ends(ends, step)

        def put(j, first, second, last, z=z, pitch=pitch, n=n, r=r):
            for at, row in ((8 + n, first), (10 + n, second), (6, last)):
                z[pl.ds(j * pitch + at, 1)] = r[row : row + 1]

        for j in range(n):
            if lev == 0:
                at = (j // 2) * 8 + 5 * (j % 2)
                put(j + 2, at, at + 1, at + 2)
            elif lev == 1:
                put(j + 2, j * 8, j * 8 + 3, j * 8 + 4)
            else:
                put(j + 2, j * 16, 128 + 2 * j, 129 + 2 * j)
        put(n + 2, 18 * 8, 18 * 8 + 1 + lev, 18 * 8 + 6 - lev)
        at = (19 + lev) * 8
        put(n + 4, at, at + 1, at + 2)
        put(0, at + 3, at + 4, at + 5)

    def lift_plane(z, pitch, p):
        def plane(q):
            return z[pl.ds(pl.multiple_of(q * pitch, 8), pitch)]

        z[pl.ds(pl.multiple_of(p * pitch, 8), pitch)] = plane(p) - predicted(
            plane(p - 3), plane(p - 1), plane(p + 1), plane(p + 3)
        )

    def lift1(k, _):
        lift_plane(z1, 48, 2 * k + 3)
        return _

    lax.fori_loop(0, 16, lift1, 0, unroll=2)
    for k in range(8):
        lift_plane(z2, 32, 2 * k + 3)
    for k in range(4):
        lift_plane(z3, 24, 2 * k + 3)

    def lifted(load, count):
        low = [load(2 * j) for j in range(-1, count + 2)]
        high = [
            load(2 * j + 1) - predicted(low[j], low[j + 1], low[j + 2], low[j + 3])
            for j in range(count)
        ]
        return low[1 : count + 1], high

    parts = []
    for hx in range(2):
        sides = lifted(
            lambda y: z1[pl.ds((2 + hx) * 48 + 8 + y, 16, stride=96), :], 16
        )
        for side in sides:
            for top in range(2):
                tiles = [v.astype(BF16) for v in side[8 * top : 8 * top + 8]]
                parts.append(jnp.concatenate(tiles, axis=1))
    made = dot(jnp.concatenate(parts, axis=0), sort1[...])
    for c in range(8):
        for r in range(8):
            at = field * 1024 + ((c // 2) * 8 + r) * 32 + c % 2
            st1[pl.ds(at, 16, stride=2), :] = made[16 * c : 16 * c + 16, 128 * r : 128 * r + 128]

    even_lane = lanes(8) % 2 == 0
    parts = []
    for hx in range(2):
        sides = lifted(
            lambda y: z2[pl.ds((2 + hx) * 32 + 8 + y, 8, stride=64), :], 8
        )
        for side in sides:
            tiles = []
            for v in side:
                after = pltpu.roll(pltpu.roll(v, 7, 0), 1, 1)
                tiles.append(jnp.where(even_lane, v, after))
            parts.append(jnp.concatenate(tiles, axis=1))
    in2[pl.ds(pl.multiple_of(field * 32, 32), 32)] = jnp.concatenate(parts, axis=0).astype(BF16)

    lane8 = lanes(8)
    tiles = []
    for hx in range(2):
        acc = [None, None]
        for k in range(4):
            base = (2 * k + 2 + hx) * 24

            def rows_from(start, base=base):
                return z3[pl.ds(base + start, 4, stride=2), :]

            low = rows_from(8)
            high = rows_from(9) - predicted(rows_from(6), low, rows_from(10), rows_from(12))
            for hy, side in enumerate((low, high)):
                if k == 0:
                    acc[hy] = side
                else:
                    acc[hy] = jnp.where(lanes(4) % 4 == k, pltpu.roll(side, k, 1), acc[hy])
        t3[pl.ds(0, 4)] = acc[0]
        t3[pl.ds(4, 4)] = acc[1]
        tiles.append(shuffle(t3[pl.ds(0, 8)], shuffle_indices()))
    left = lane8 < 64
    a, c = tiles
    ar, cr = pltpu.roll(a, 64, 1), pltpu.roll(c, 64, 1)

    def above(t):
        return pltpu.roll(t, 1, 0)

    groups = (
        jnp.where(left, above(a), 0.0),
        jnp.where(left, a, above(a)),
        jnp.where(left, ar, above(cr)),
        jnp.where(left, c, above(c)),
        jnp.where(left, cr, 0.0),
    )
    for b in range(NB):
        for j, group in enumerate(groups):
            st3[pl.ds(field * 32 + b * 8 + j, 1)] = group[2 * b + 1 : 2 * b + 2]

    @pl.when(field == NF - 1)
    def _():
        made = dot(in2[...], sort2[...])
        for r in range(8):
            out2[r] = made[:, 128 * r : 128 * r + 128]
        total = lax.fori_loop(0, me[0], lambda i, s: s + cnt[i], jnp.int32(0))
        first = total % CAP

        def one(f, here):
            for b in range(NB):
                flags = [ret[(b * NF + f) * 3 + lev] for lev in range(3)]
                ring[pl.ds(here, 8)] = st3[pl.ds(pl.multiple_of(f * 32 + b * 8, 8), 8)]
                at2 = here + P0 + P3 * flags[2]
                at1 = at2 + P2 * flags[1]
                here = at1 + P1 * flags[0]

                @pl.when(flags[1] > 0)
                def _(b=b, at2=at2):
                    for s in range(1, 8):
                        r = b * 2 + s % 2
                        ring[pl.ds(at2 + (s - 1) * 4, 4)] = out2[
                            r, pl.ds(f * 32 + (s // 2) * 8, 4, stride=2), :
                        ]

                @pl.when(flags[0] > 0)
                def _(b=b, at1=at1):
                    for s in range(1, 8):
                        start = f * 1024 + ((s // 2) * 8 + b * 2 + s % 2) * 32
                        ring[pl.ds(at1 + (s - 1) * 32, 32)] = st1[
                            pl.ds(pl.multiple_of(start, 32), 32)
                        ]
            return here

        lax.fori_loop(0, NF, one, first)
        used = -(-CAP // rows)

        def fold(i, _):
            at = pl.multiple_of(i * rows, 8)
            near, far = ring[pl.ds(at, rows)], ring[pl.ds(at + CAP, rows)]
            out[i] = jnp.where(at + subs(rows) >= first, near, far).astype(BF16)
            return _

        lax.fori_loop(0, used, fold, 0)
        for block in range(used, nblk):
            out[block] = jnp.zeros((rows, 128), BF16)


def transform(me, counts, flags, fields, halos, blocks, rows):
    shapes = ((32, 32, 128),) + tuple(h.shape[1:] for h in halos)
    ring_rows = (2 * CAP + rows + 135) // 8 * 8
    return pl.pallas_call(
        main_kernel,
        grid=(NF,),
        in_specs=[smem(), smem(), smem()] + [field_block(*shape) for shape in shapes],
        out_specs=pl.BlockSpec((blocks, rows, 128), lambda f: (0, 0, 0)),
        out_shape=jax.ShapeDtypeStruct((blocks, rows, 128), BF16),
        scratch_shapes=[
            pltpu.VMEM((37 * 48, 128), F32),
            pltpu.VMEM((21 * 32, 128), F32),
            pltpu.VMEM((13 * 24, 128), F32),
            pltpu.VMEM((NF * 32, 1024), BF16),
            pltpu.VMEM((8, NF * 32, 128), F32),
            pltpu.VMEM((NF * 1024, 128), F32),
            pltpu.VMEM((NF * 32, 128), F32),
            pltpu.VMEM((32, 128), F32),
            pltpu.VMEM((ring_rows, 128), F32),
            pltpu.VMEM((384, 384), BF16),
            pltpu.VMEM((1024, 1024), BF16),
            pltpu.VMEM((1024, 1024), BF16),
        ],
        compiler_params=pltpu.CompilerParams(vmem_limit_bytes=48 * 2**20),
        name="transform",
    )(me, counts, flags, fields, *halos)


def route_kernel(me, cnt, recv, send):
    n, rows = recv.shape[0], recv.shape[1]
    slot = me[0] * rows + subs(rows)
    send[...] = jnp.zeros_like(send)

    def one(i, begin):
        count = cnt[i]
        place, first = begin // CAP, begin % CAP
        end = first + count
        value = recv[i]
        here = (slot >= first) & (slot < jnp.minimum(end, CAP))
        send[place] = jnp.where(here, value, send[place])

        @pl.when(end > CAP)
        def _():
            send[place + 1] = jnp.where(slot < end - CAP, value, send[place + 1])

        return begin + count

    lax.fori_loop(0, n, one, jnp.int32(0))


def route(me, counts, received):
    return pl.pallas_call(
        route_kernel,
        in_specs=[smem(), smem(), pl.BlockSpec(memory_space=pltpu.VMEM)],
        out_specs=pl.BlockSpec(memory_space=pltpu.VMEM),
        out_shape=jax.ShapeDtypeStruct(received.shape, BF16),
        compiler_params=pltpu.CompilerParams(vmem_limit_bytes=40 * 2**20),
        name="route",
    )(me, counts, received)


def swapped(value, n, axis, dy=0, dz=0):
    pairs = []
    for x in range(n):
        to = (x, x ^ 1, (x + 1 if x % 2 else x - 1) % n)[axis]
        for y in range(2):
            for z in range(2):
                there = (to * 2 + (y + dy) % 2) * 2 + (z + dz) % 2
                pairs.append(((x * 2 + y) * 2 + z, there))
    return lax.ppermute(value, ("gx", "gy", "gz"), pairs)


def per_device(n, fields, retained):
    me = lax.axis_index("gx").astype(jnp.int32).reshape(1)
    odd = me % 2
    flags = retained.reshape(-1)
    core, other = boundary_planes(odd, fields)
    core, other = swapped(core, n, 1), swapped(other, n, 2)
    yy, zz, yz, place = pack(me, flags, fields, core, other, n)
    counts = lax.psum(place, "gx")
    halos = (
        core,
        other,
        swapped(yy, n, 0, dy=1),
        swapped(zz, n, 0, dz=1),
        swapped(yz, n, 0, dy=1, dz=1),
    )
    rows = -(-CAP // (8 * n)) * 8
    ring = transform(me, counts, flags, fields, halos, n, rows)
    spread = lax.all_to_all(ring, "gx", 0, 0, tiled=True)
    routed = route(me, counts, spread)
    stream = lax.all_to_all(routed, "gx", 0, 0, tiled=True)
    return stream.reshape(1, 1, n * rows, 128)[:, :, :CAP]


def solution(mesh):
    placed = (P(None, "gx", "gy", "gz"), P("gx", "gy", "gz", None, None))
    return jax.shard_map(
        functools.partial(per_device, mesh.shape["gx"]),
        mesh=mesh,
        in_specs=placed,
        out_specs=P("gy", "gz", "gx", None),
        check_vma=False,
    )
```

```python
import functools

import jax
import jax.numpy as jnp
from jax import lax
from jax.experimental import pallas as pl
from jax.experimental.pallas import tpu as pltpu
from jax.sharding import PartitionSpec as P

P1 = 224
P2 = 28
P3 = 4
P0 = 1
CAP = 7196
NF = 7
NB = 4
F32 = jnp.float32
BF16 = jnp.bfloat16
W9 = 9.0 / 16.0
W1 = 1.0 / 16.0

LEVEL_ROWS = ((0, 2, 30), (0, 4, 28), (0, 8, 24))
PAIR = (0, 2, 30, 4, 28, 0, 2, 30)
CORNERS = (
    tuple((0, row) for row in (0, 2, 4, 8, 24, 28, 30, 30)),
    tuple((1, row) for row in (0, 2, 30)) + tuple((6, row) for row in (0, 2, 30, 30, 30)),
    tuple((2, row) for row in (0, 4, 28)) + tuple((5, row) for row in (0, 4, 28, 28, 28)),
    tuple((3, row) for row in (0, 8, 24)) + tuple((4, row) for row in (0, 8, 24, 24, 24)),
)
TILES = 22


def lanes(rows, width=128):
    return lax.broadcasted_iota(jnp.int32, (rows, width), 1)


def subs(rows, width=128):
    return lax.broadcasted_iota(jnp.int32, (rows, width), 0)


def thirds(v):
    high = v.astype(BF16)
    rest = v - high.astype(F32)
    mid = rest.astype(BF16)
    low = (rest - mid.astype(F32)).astype(BF16)
    return jnp.concatenate([high, mid, low], axis=1)


def dot(a, b):
    return jnp.dot(a, b, preferred_element_type=F32)


def field_block(*shape):
    return pl.BlockSpec((1,) + shape, lambda f, *_: (f,) + (0,) * len(shape))


def smem():
    return pl.BlockSpec(memory_space=pltpu.SMEM)


def planes_kernel(odd, *refs):
    core, other = refs[8:]
    for k in range(4):
        core[:, k] = refs[2 * k][:, 0]
        other[:, k] = refs[2 * k + 1][:, 0]


def boundary_planes(odd, fields):
    def block(k, j):
        high, low = (1 << k) & 14, 32 - (8 >> k)
        return pl.BlockSpec(
            (NF, 1, 32, 128),
            lambda i, odd: (0, jnp.where(odd[0] == 1 - j, high, low), 0, 0),
        )

    shape = (NF, 4, 32, 128)
    return pl.pallas_call(
        planes_kernel,
        grid_spec=pltpu.PrefetchScalarGridSpec(
            num_scalar_prefetch=1,
            grid=(1,),
            in_specs=[block(k, j) for k in range(4) for j in range(2)],
            out_specs=[pl.BlockSpec(shape, lambda i, odd: (0, 0, 0, 0))] * 2,
        ),
        out_shape=[jax.ShapeDtypeStruct(shape, F32)] * 2,
        name="planes",
    )(odd, *[fields] * 8)


def halo_plane(odd, core, other, p):
    if p < 4:
        return jnp.where(odd == 1, other[0, p], core[0, p])
    return jnp.where(odd == 1, core[0, p - 4], other[0, p - 4])


END_A = (0, 0, 0, 0, 124, 126, 120, 0)
END_B = (4, 0, 8, 2, 0, 0, 0, 0)


def pack_kernel(me, ret, f_ref, core, other, yy, zz, yz, count, ends):
    odd = me[0] % 2

    @pl.when(pl.program_id(0) == 0)
    def _():
        live = jnp.int32(NB * NF * P0)
        for i in range(NB * NF):
            live = live + ret[3 * i] * P1 + ret[3 * i + 1] * P2 + ret[3 * i + 2] * P3
        for i in range(count.shape[0]):
            count[i] = jnp.where(me[0] == i, live, 0)
        lane, row = lanes(384) % 8, subs(384) % 128
        weight = jnp.zeros((384, 128), F32)
        for col in range(7):
            joint = col in (0, 2, 3)
            weight = jnp.where((lane == col) & (row == END_A[col]), W9 if joint else -W1, weight)
            if joint:
                weight = jnp.where((lane == col) & (row == END_B[col]), -W1, weight)
        ends[...] = weight.astype(BF16)

    chunk = lanes(32) // 8
    weight = ends[...]
    for part in range(3):
        if part < 2:
            planes = [f_ref[0, part * 16 + k] for k in range(16)]
        else:
            planes = [halo_plane(odd, core, other, p) for p in range(7)]
        made = dot(thirds(jnp.concatenate(planes, axis=0)), weight)
        acc = jnp.zeros((32, 128), F32)
        for k in range(len(planes)):
            acc = jnp.where(chunk == k, made[32 * k : 32 * k + 32], acc)
        zz[0, part] = acc

    for half in range(2):
        for j, row in enumerate(PAIR):
            yz[0, half, j] = zz[0, half, row]
        for j in range(8):
            yz[0, 2 + half, j] = zz[0, half, 8 if j % 2 == 0 else 24]
    for t, corner in enumerate(CORNERS):
        for j, (_, row) in enumerate(corner):
            yz[0, 4 + t, j] = zz[0, 2, row]

    for k in range(16):
        for j, row in enumerate(PAIR):
            yy[0, k, j] = f_ref[0, 2 * k + (j >= 5), row]
    for k in range(8):
        for j in range(2):
            yy[0, 16 + k // 4, (k % 4) * 2 + j] = f_ref[0, 4 * k, (8, 24)[j]]
    whole = [halo_plane(odd, core, other, p) for p in range(7)]
    for t, corner in enumerate(CORNERS):
        for j, (p, row) in enumerate(corner):
            yy[0, 18 + t, j] = whole[p][row]


def pack(me, flags, fields, core, other, n):
    shapes = ((TILES, 8, 128), (3, 32, 128), (8, 8, 128))
    return pl.pallas_call(
        pack_kernel,
        grid=(NF,),
        in_specs=[smem(), smem(), field_block(32, 32, 128)] + [field_block(4, 32, 128)] * 2,
        out_specs=[field_block(*shape) for shape in shapes] + [smem()],
        out_shape=[jax.ShapeDtypeStruct((NF,) + shape, F32) for shape in shapes]
        + [jax.ShapeDtypeStruct((n,), jnp.int32)],
        scratch_shapes=[pltpu.VMEM((384, 128), BF16)],
        compiler_params=pltpu.CompilerParams(vmem_limit_bytes=40 * 2**20),
        name="pack",
    )(me, flags, fields, core, other)


STEPS = (1, 2, 4)


def lift_matrix(step):
    row, lane = subs(384) % 128, lanes(384)
    odd = lane % (2 * step) == step
    apart = jnp.abs(row - lane)
    weight = jnp.where(odd & (apart == step), -W9, 0.0)
    weight = jnp.where(odd & (apart == 3 * step), W1, weight)
    return jnp.where(apart == 0, 1.0, weight).astype(BF16)


def at_ends(ends, step):
    lane = lanes(ends.shape[0])
    edge = (lane == step) | (lane == 128 - step) | (lane == 128 - 3 * step)
    return jnp.where(edge, ends, 0.0)


def end_index(rows):
    lane = lanes(rows)
    index = jnp.ones_like(lane)
    for at, col in ((126, 0), (124, 2), (127, 3), (2, 4), (1, 5), (4, 6)):
        index = jnp.where(lane == at, col, index)
    return index


def predicted(a, b, c, d):
    return W9 * (b + c) - W1 * (a + d)


def pick(values, index):
    return jnp.take_along_axis(values, index, axis=1)


def packet_matrix(level, y):
    lane, col = subs(128, 1024), lanes(128, 1024)
    r, at = col // 128, col % 128
    b, hz = r // 2, r % 2
    if level == 1:
        source, row = b * 32 + (at % 16) * 2 + hz, at // 16
    else:
        source = b * 32 + (at % 8) * 4 + hz * 2 + at // 64
        row = (at // 8) % 8
    return jnp.where((lane == source) & (row == y), 1.0, 0.0).astype(BF16)


def shuffle_indices():
    lane, sub = lanes(8), subs(8)
    r = (lane // 16 - sub) % 8
    w = lane % 16
    first = (r // 2) * 32 + (w % 4) * 8 + (r % 2) * 4 + w // 4
    y = (lane // 64) * 4 + (lane // 4) % 4
    rest = ((lane // 16) % 4) * 4 + lane % 4
    return first, r, ((y + sub) % 8) * 16 + rest


def shuffle(tile, indices):
    first, middle, last = indices
    tile = jnp.take_along_axis(tile, first, axis=1)
    tile = jnp.take_along_axis(tile, middle, axis=0)
    return jnp.take_along_axis(tile, last, axis=1)


def main_kernel(
    me, cnt, ret, f_ref, core, other, yy, zz, yz,
    out, z1, z2, z3, in2, out2, st1, st3, t3, ring, lifts, sort1, sort2,
):
    field = pl.program_id(0)
    nblk, rows = out.shape[0], out.shape[1]
    odd = me[0] % 2

    @pl.when(field == 0)
    def _():
        for lev, step in enumerate(STEPS):
            lifts[:, lev * 128 : lev * 128 + 128] = lift_matrix(step)
        for y in range(8):
            sort1[y * 128 : y * 128 + 128] = packet_matrix(1, y)
            sort2[y * 128 : y * 128 + 128] = packet_matrix(2, y)

    weight = lifts[:, 0:128]
    for g in range(4):
        made = dot(thirds(f_ref[0, 8 * g : 8 * g + 8].reshape(256, 128)), weight)
        for k in range(8):
            x = 8 * g + k
            e = pltpu.roll(zz[0, x // 16], (124 - 8 * (x % 16)) % 128, 1)
            z1[pl.ds((x + 2) * 48 + 8, 32)] = made[32 * k : 32 * k + 32] - at_ends(e, 1)

    def cells(lev, x):
        step = STEPS[lev]
        return f_ref[0, x, pl.ds(0, 32 // step, stride=step), :]

    def ends_of(lev, part, k):
        step = STEPS[lev]
        n = 32 // step
        e = zz[0, part, pl.ds(0, n, stride=step), :] if step > 1 else zz[0, part]
        return at_ends(pick(e, end_index(n) + 8 * k), step)

    for lev, z, to in ((1, z2, lambda j: j * 32 + 8), (2, z3, lambda j: j * 24 + 8)):
        step = STEPS[lev]
        n = 32 // step
        v = jnp.concatenate([cells(lev, j * step) for j in range(n)], axis=0)
        made = dot(thirds(v), lifts[:, lev * 128 : lev * 128 + 128])
        for j in range(n):
            x = j * step
            z[pl.ds(to(j + 2), n)] = made[n * j : n * j + n] - ends_of(lev, x // 16, x % 16)

    def halo_cells(p, step):
        first, second, q = (other, core, p) if p < 4 else (core, other, p - 4)
        if step == 1:
            return jnp.where(odd == 1, first[0, q], second[0, q])
        some = pl.ds(0, 32 // step, stride=step)
        return jnp.where(odd == 1, first[0, q, some, :], second[0, q, some, :])

    for lev, (z, pitch) in enumerate(((z1, 48), (z2, 32), (z3, 24))):
        step = STEPS[lev]
        n = 32 // step
        which = ((0, n + 2), (1 + lev, n + 4), (6 - lev, 0))
        v = jnp.concatenate([halo_cells(p, step) for p, _ in which], axis=0)
        made = dot(thirds(v), lifts[:, lev * 128 : lev * 128 + 128])
        for k, (p, at) in enumerate(which):
            z[pl.ds(at * pitch + 8, n)] = made[n * k : n * k + n] - ends_of(lev, 2, p)

    made = dot(thirds(yy[0].reshape(TILES * 8, 128)), lifts[...])
    sub, index = subs(8), end_index(8)
    ends = []
    for t in range(TILES):
        if t < 16:
            e, chunk = yz[0, t // 8], jnp.where(sub < 5, 2 * t % 16, (2 * t + 1) % 16)
        elif t < 18:
            e, chunk = yz[0, 2 + t - 16], (sub // 2) * 4
        elif t == 18:
            e, chunk = yz[0, 4], 0
        else:
            e, chunk = yz[0, t - 14], jnp.where(sub < 3, t - 18, 25 - t)
        ends.append(pick(e, index + 8 * chunk))
    ends = jnp.concatenate(ends, axis=0)
    for lev, (z, pitch) in enumerate(((z1, 48), (z2, 32), (z3, 24))):
        step = STEPS[lev]
        n = 32 // step
        r = made[:, lev * 128 : lev * 128 + 128] - at_ends(ends, step)

        def put(j, first, second, last, z=z, pitch=pitch, n=n, r=r):
            for at, row in ((8 + n, first), (10 + n, second), (6, last)):
                z[pl.ds(j * pitch + at, 1)] = r[row : row + 1]

        for j in range(n):
            if lev == 0:
                at = (j // 2) * 8 + 5 * (j % 2)
                put(j + 2, at, at + 1, at + 2)
            elif lev == 1:
                put(j + 2, j * 8, j * 8 + 3, j * 8 + 4)
            else:
                put(j + 2, j * 16, 128 + 2 * j, 129 + 2 * j)
        put(n + 2, 18 * 8, 18 * 8 + 1 + lev, 18 * 8 + 6 - lev)
        at = (19 + lev) * 8
        put(n + 4, at, at + 1, at + 2)
        put(0, at + 3, at + 4, at + 5)

    def lift_plane(z, pitch, p):
        def plane(q):
            return z[pl.ds(pl.multiple_of(q * pitch, 8), pitch)]

        z[pl.ds(pl.multiple_of(p * pitch, 8), pitch)] = plane(p) - predicted(
            plane(p - 3), plane(p - 1), plane(p + 1), plane(p + 3)
        )

    def lift1(k, _):
        lift_plane(z1, 48, 2 * k + 3)
        return _

    lax.fori_loop(0, 16, lift1, 0, unroll=True)
    for k in range(8):
        lift_plane(z2, 32, 2 * k + 3)
    for k in range(4):
        lift_plane(z3, 24, 2 * k + 3)

    def lifted(load, count):
        low = [load(2 * j) for j in range(-1, count + 2)]
        high = [
            load(2 * j + 1) - predicted(low[j], low[j + 1], low[j + 2], low[j + 3])
            for j in range(count)
        ]
        return low[1 : count + 1], high

    parts = []
    for hx in range(2):
        sides = lifted(
            lambda y: z1[pl.ds((2 + hx) * 48 + 8 + y, 16, stride=96), :], 16
        )
        for side in sides:
            for top in range(2):
                tiles = [v.astype(BF16) for v in side[8 * top : 8 * top + 8]]
                parts.append(jnp.concatenate(tiles, axis=1))
    made = dot(jnp.concatenate(parts, axis=0), sort1[...])
    for c in range(8):
        for r in range(8):
            at = field * 1024 + ((c // 2) * 8 + r) * 32 + c % 2
            st1[pl.ds(at, 16, stride=2), :] = made[16 * c : 16 * c + 16, 128 * r : 128 * r + 128]

    even_lane = lanes(8) % 2 == 0
    parts = []
    for hx in range(2):
        sides = lifted(
            lambda y: z2[pl.ds((2 + hx) * 32 + 8 + y, 8, stride=64), :], 8
        )
        for side in sides:
            tiles = []
            for v in side:
                after = pltpu.roll(pltpu.roll(v, 7, 0), 1, 1)
                tiles.append(jnp.where(even_lane, v, after))
            parts.append(jnp.concatenate(tiles, axis=1))
    in2[pl.ds(pl.multiple_of(field * 32, 32), 32)] = jnp.concatenate(parts, axis=0).astype(BF16)

    lane8 = lanes(8)
    tiles = []
    for hx in range(2):
        acc = [None, None]
        for k in range(4):
            base = (2 * k + 2 + hx) * 24

            def rows_from(start, base=base):
                return z3[pl.ds(base + start, 4, stride=2), :]

            low = rows_from(8)
            high = rows_from(9) - predicted(rows_from(6), low, rows_from(10), rows_from(12))
            for hy, side in enumerate((low, high)):
                if k == 0:
                    acc[hy] = side
                else:
                    acc[hy] = jnp.where(lanes(4) % 4 == k, pltpu.roll(side, k, 1), acc[hy])
        t3[pl.ds(0, 4)] = acc[0]
        t3[pl.ds(4, 4)] = acc[1]
        tiles.append(shuffle(t3[pl.ds(0, 8)], shuffle_indices()))
    left = lane8 < 64
    a, c = tiles
    ar, cr = pltpu.roll(a, 64, 1), pltpu.roll(c, 64, 1)

    def above(t):
        return pltpu.roll(t, 1, 0)

    groups = (
        jnp.where(left, above(a), 0.0),
        jnp.where(left, a, above(a)),
        jnp.where(left, ar, above(cr)),
        jnp.where(left, c, above(c)),
        jnp.where(left, cr, 0.0),
    )
    for b in range(NB):
        for j, group in enumerate(groups):
            st3[pl.ds(field * 32 + b * 8 + j, 1)] = group[2 * b + 1 : 2 * b + 2]

    @pl.when(field == NF - 1)
    def _():
        made = dot(in2[...], sort2[...])
        for r in range(8):
            out2[r] = made[:, 128 * r : 128 * r + 128]
        total = lax.fori_loop(0, me[0], lambda i, s: s + cnt[i], jnp.int32(0))
        first = total % CAP

        def one(f, here):
            for b in range(NB):
                flags = [ret[(b * NF + f) * 3 + lev] for lev in range(3)]
                ring[pl.ds(here, 8)] = st3[pl.ds(pl.multiple_of(f * 32 + b * 8, 8), 8)]
                at2 = here + P0 + P3 * flags[2]
                at1 = at2 + P2 * flags[1]
                here = at1 + P1 * flags[0]

                @pl.when(flags[1] > 0)
                def _(b=b, at2=at2):
                    for s in range(1, 8):
                        r = b * 2 + s % 2
                        ring[pl.ds(at2 + (s - 1) * 4, 4)] = out2[
                            r, pl.ds(f * 32 + (s // 2) * 8, 4, stride=2), :
                        ]

                @pl.when(flags[0] > 0)
                def _(b=b, at1=at1):
                    for s in range(1, 8):
                        start = f * 1024 + ((s // 2) * 8 + b * 2 + s % 2) * 32
                        ring[pl.ds(at1 + (s - 1) * 32, 32)] = st1[
                            pl.ds(pl.multiple_of(start, 32), 32)
                        ]
            return here

        lax.fori_loop(0, NF, one, first)
        used = -(-CAP // rows)

        def fold(i, _):
            at = pl.multiple_of(i * rows, 8)
            near, far = ring[pl.ds(at, rows)], ring[pl.ds(at + CAP, rows)]
            out[i] = jnp.where(at + subs(rows) >= first, near, far).astype(BF16)
            return _

        lax.fori_loop(0, used, fold, 0, unroll=4)
        for block in range(used, nblk):
            out[block] = jnp.zeros((rows, 128), BF16)


def transform(me, counts, flags, fields, halos, blocks, rows):
    shapes = ((32, 32, 128),) + tuple(h.shape[1:] for h in halos)
    ring_rows = (2 * CAP + rows + 135) // 8 * 8
    return pl.pallas_call(
        main_kernel,
        grid=(NF,),
        in_specs=[smem(), smem(), smem()] + [field_block(*shape) for shape in shapes],
        out_specs=pl.BlockSpec((blocks, rows, 128), lambda f: (0, 0, 0)),
        out_shape=jax.ShapeDtypeStruct((blocks, rows, 128), BF16),
        scratch_shapes=[
            pltpu.VMEM((37 * 48, 128), F32),
            pltpu.VMEM((21 * 32, 128), F32),
            pltpu.VMEM((13 * 24, 128), F32),
            pltpu.VMEM((NF * 32, 1024), BF16),
            pltpu.VMEM((8, NF * 32, 128), F32),
            pltpu.VMEM((NF * 1024, 128), F32),
            pltpu.VMEM((NF * 32, 128), F32),
            pltpu.VMEM((32, 128), F32),
            pltpu.VMEM((ring_rows, 128), F32),
            pltpu.VMEM((384, 384), BF16),
            pltpu.VMEM((1024, 1024), BF16),
            pltpu.VMEM((1024, 1024), BF16),
        ],
        compiler_params=pltpu.CompilerParams(vmem_limit_bytes=48 * 2**20),
        name="transform",
    )(me, counts, flags, fields, *halos)


def route_kernel(me, cnt, recv, send):
    n, rows = recv.shape[0], recv.shape[1]
    slot = me[0] * rows + subs(rows)
    send[...] = jnp.zeros_like(send)

    def one(i, begin):
        count = cnt[i]
        place, first = begin // CAP, begin % CAP
        end = first + count
        value = recv[i]
        here = (slot >= first) & (slot < jnp.minimum(end, CAP))
        send[place] = jnp.where(here, value, send[place])

        @pl.when(end > CAP)
        def _():
            send[place + 1] = jnp.where(slot < end - CAP, value, send[place + 1])

        return begin + count

    lax.fori_loop(0, n, one, jnp.int32(0), unroll=4)


def route(me, counts, received):
    return pl.pallas_call(
        route_kernel,
        in_specs=[smem(), smem(), pl.BlockSpec(memory_space=pltpu.VMEM)],
        out_specs=pl.BlockSpec(memory_space=pltpu.VMEM),
        out_shape=jax.ShapeDtypeStruct(received.shape, BF16),
        compiler_params=pltpu.CompilerParams(vmem_limit_bytes=40 * 2**20),
        name="route",
    )(me, counts, received)


def swapped(value, n, axis, dy=0, dz=0):
    pairs = []
    for x in range(n):
        to = (x, x ^ 1, (x + 1 if x % 2 else x - 1) % n)[axis]
        for y in range(2):
            for z in range(2):
                there = (to * 2 + (y + dy) % 2) * 2 + (z + dz) % 2
                pairs.append(((x * 2 + y) * 2 + z, there))
    return lax.ppermute(value, ("gx", "gy", "gz"), pairs)


def per_device(n, fields, retained):
    me = lax.axis_index("gx").astype(jnp.int32).reshape(1)
    odd = me % 2
    flags = retained.reshape(-1)
    core, other = boundary_planes(odd, fields)
    core, other = swapped(core, n, 1), swapped(other, n, 2)
    yy, zz, yz, place = pack(me, flags, fields, core, other, n)
    counts = lax.psum(place, "gx")
    halos = (
        core,
        other,
        swapped(yy, n, 0, dy=1),
        swapped(zz, n, 0, dz=1),
        swapped(yz, n, 0, dy=1, dz=1),
    )
    rows = -(-CAP // (8 * n)) * 8
    ring = transform(me, counts, flags, fields, halos, n, rows)
    spread = lax.all_to_all(ring, "gx", 0, 0, tiled=True)
    routed = route(me, counts, spread)
    stream = lax.all_to_all(routed, "gx", 0, 0, tiled=True)
    return stream.reshape(1, 1, n * rows, 128)[:, :, :CAP]


def solution(mesh):
    placed = (P(None, "gx", "gy", "gz"), P("gx", "gy", "gz", None, None))
    return jax.shard_map(
        functools.partial(per_device, mesh.shape["gx"]),
        mesh=mesh,
        in_specs=placed,
        out_specs=P("gy", "gz", "gx", None),
        check_vma=False,
    )
```

```python
import functools

import jax
import jax.numpy as jnp
from jax import lax
from jax.experimental import pallas as pl
from jax.experimental.pallas import tpu as pltpu
from jax.sharding import PartitionSpec as P

P1 = 224
P2 = 28
P3 = 4
P0 = 1
CAP = 7196
NF = 7
NB = 4
F32 = jnp.float32
BF16 = jnp.bfloat16
W9 = 9.0 / 16.0
W1 = 1.0 / 16.0

LEVEL_ROWS = ((0, 2, 30), (0, 4, 28), (0, 8, 24))
PAIR = (0, 2, 30, 4, 28, 0, 2, 30)
CORNERS = (
    tuple((0, row) for row in (0, 2, 4, 8, 24, 28, 30, 30)),
    tuple((1, row) for row in (0, 2, 30)) + tuple((6, row) for row in (0, 2, 30, 30, 30)),
    tuple((2, row) for row in (0, 4, 28)) + tuple((5, row) for row in (0, 4, 28, 28, 28)),
    tuple((3, row) for row in (0, 8, 24)) + tuple((4, row) for row in (0, 8, 24, 24, 24)),
)
TILES = 22


def lanes(rows, width=128):
    return lax.broadcasted_iota(jnp.int32, (rows, width), 1)


def subs(rows, width=128):
    return lax.broadcasted_iota(jnp.int32, (rows, width), 0)


def thirds(v):
    high = v.astype(BF16)
    rest = v - high.astype(F32)
    mid = rest.astype(BF16)
    low = (rest - mid.astype(F32)).astype(BF16)
    return jnp.concatenate([high, mid, low], axis=1)


def dot(a, b):
    return jnp.dot(a, b, preferred_element_type=F32)


def field_block(*shape):
    return pl.BlockSpec((1,) + shape, lambda f, *_: (f,) + (0,) * len(shape))


def smem():
    return pl.BlockSpec(memory_space=pltpu.SMEM)


def planes_kernel(odd, *refs):
    core, other = refs[8:]
    for k in range(4):
        core[:, k] = refs[2 * k][:, 0]
        other[:, k] = refs[2 * k + 1][:, 0]


def boundary_planes(odd, fields):
    def block(k, j):
        high, low = (1 << k) & 14, 32 - (8 >> k)
        return pl.BlockSpec(
            (NF, 1, 32, 128),
            lambda i, odd: (0, jnp.where(odd[0] == 1 - j, high, low), 0, 0),
        )

    shape = (NF, 4, 32, 128)
    return pl.pallas_call(
        planes_kernel,
        grid_spec=pltpu.PrefetchScalarGridSpec(
            num_scalar_prefetch=1,
            grid=(1,),
            in_specs=[block(k, j) for k in range(4) for j in range(2)],
            out_specs=[pl.BlockSpec(shape, lambda i, odd: (0, 0, 0, 0))] * 2,
        ),
        out_shape=[jax.ShapeDtypeStruct(shape, F32)] * 2,
        name="planes",
    )(odd, *[fields] * 8)


def halo_plane(odd, core, other, p):
    if p < 4:
        return jnp.where(odd == 1, other[0, p], core[0, p])
    return jnp.where(odd == 1, core[0, p - 4], other[0, p - 4])


END_A = (0, 0, 0, 0, 124, 126, 120, 0)
END_B = (4, 0, 8, 2, 0, 0, 0, 0)


def pack_kernel(me, ret, f_ref, core, other, yy, zz, yz, count, ends):
    odd = me[0] % 2

    @pl.when(pl.program_id(0) == 0)
    def _():
        kept = [sum(ret[3 * i + lev] for i in range(NB * NF)) for lev in range(3)]
        for i in range(count.shape[0]):
            count[i] = jnp.int32(0)
        count[me[0]] = NB * NF * P0 + kept[0] * P1 + kept[1] * P2 + kept[2] * P3
        lane, row = lanes(384) % 8, subs(384) % 128
        weight = jnp.zeros((384, 128), F32)
        for col in range(7):
            joint = col in (0, 2, 3)
            weight = jnp.where((lane == col) & (row == END_A[col]), W9 if joint else -W1, weight)
            if joint:
                weight = jnp.where((lane == col) & (row == END_B[col]), -W1, weight)
        ends[...] = weight.astype(BF16)

    chunk = lanes(32) // 8
    weight = ends[...]
    for part in range(3):
        if part < 2:
            planes = [f_ref[0, part * 16 + k] for k in range(16)]
        else:
            planes = [halo_plane(odd, core, other, p) for p in range(7)]
        made = dot(thirds(jnp.concatenate(planes, axis=0)), weight)
        acc = jnp.zeros((32, 128), F32)
        for k in range(len(planes)):
            acc = jnp.where(chunk == k, made[32 * k : 32 * k + 32], acc)
        zz[0, part] = acc

    for half in range(2):
        for j, row in enumerate(PAIR):
            yz[0, half, j] = zz[0, half, row]
        for j in range(8):
            yz[0, 2 + half, j] = zz[0, half, 8 if j % 2 == 0 else 24]
    for t, corner in enumerate(CORNERS):
        for j, (_, row) in enumerate(corner):
            yz[0, 4 + t, j] = zz[0, 2, row]

    for k in range(16):
        for j, row in enumerate(PAIR):
            yy[0, k, j] = f_ref[0, 2 * k + (j >= 5), row]
    for k in range(8):
        for j in range(2):
            yy[0, 16 + k // 4, (k % 4) * 2 + j] = f_ref[0, 4 * k, (8, 24)[j]]
    whole = [halo_plane(odd, core, other, p) for p in range(7)]
    for t, corner in enumerate(CORNERS):
        for j, (p, row) in enumerate(corner):
            yy[0, 18 + t, j] = whole[p][row]


def pack(me, flags, fields, core, other, n):
    shapes = ((TILES, 8, 128), (3, 32, 128), (8, 8, 128))
    return pl.pallas_call(
        pack_kernel,
        grid=(NF,),
        in_specs=[smem(), smem(), field_block(32, 32, 128)] + [field_block(4, 32, 128)] * 2,
        out_specs=[field_block(*shape) for shape in shapes] + [smem()],
        out_shape=[jax.ShapeDtypeStruct((NF,) + shape, F32) for shape in shapes]
        + [jax.ShapeDtypeStruct((n,), jnp.int32)],
        scratch_shapes=[pltpu.VMEM((384, 128), BF16)],
        compiler_params=pltpu.CompilerParams(vmem_limit_bytes=40 * 2**20),
        name="pack",
    )(me, flags, fields, core, other)


STEPS = (1, 2, 4)


def lift_matrix(step):
    row, lane = subs(384) % 128, lanes(384)
    odd = lane % (2 * step) == step
    apart = jnp.abs(row - lane)
    weight = jnp.where(odd & (apart == step), -W9, 0.0)
    weight = jnp.where(odd & (apart == 3 * step), W1, weight)
    return jnp.where(apart == 0, 1.0, weight).astype(BF16)


def at_ends(ends, step):
    lane = lanes(ends.shape[0])
    edge = (lane == step) | (lane == 128 - step) | (lane == 128 - 3 * step)
    return jnp.where(edge, ends, 0.0)


def end_index(rows):
    lane = lanes(rows)
    index = jnp.ones_like(lane)
    for at, col in ((126, 0), (124, 2), (127, 3), (2, 4), (1, 5), (4, 6)):
        index = jnp.where(lane == at, col, index)
    return index


def predicted(a, b, c, d):
    return W9 * (b + c) - W1 * (a + d)


def pick(values, index):
    return jnp.take_along_axis(values, index, axis=1)


def packet_matrix(level, y):
    lane, col = subs(128, 1024), lanes(128, 1024)
    r, at = col // 128, col % 128
    b, hz = r // 2, r % 2
    if level == 1:
        source, row = b * 32 + (at % 16) * 2 + hz, at // 16
    else:
        source = b * 32 + (at % 8) * 4 + hz * 2 + at // 64
        row = (at // 8) % 8
    return jnp.where((lane == source) & (row == y), 1.0, 0.0).astype(BF16)


def shuffle_indices():
    lane, sub = lanes(8), subs(8)
    r = (lane // 16 - sub) % 8
    w = lane % 16
    first = (r // 2) * 32 + (w % 4) * 8 + (r % 2) * 4 + w // 4
    y = (lane // 64) * 4 + (lane // 4) % 4
    rest = ((lane // 16) % 4) * 4 + lane % 4
    return first, r, ((y + sub) % 8) * 16 + rest


def shuffle(tile, indices):
    first, middle, last = indices
    tile = jnp.take_along_axis(tile, first, axis=1)
    tile = jnp.take_along_axis(tile, middle, axis=0)
    return jnp.take_along_axis(tile, last, axis=1)


def main_kernel(
    me, cnt, ret, f_ref, core, other, yy, zz, yz,
    out, z1, z2, z3, in2, out2, st1, st3, t3, ring, lifts, sort1, sort2,
):
    field = pl.program_id(0)
    nblk, rows = out.shape[0], out.shape[1]
    odd = me[0] % 2

    @pl.when(field == 0)
    def _():
        for lev, step in enumerate(STEPS):
            lifts[:, lev * 128 : lev * 128 + 128] = lift_matrix(step)
        for y in range(8):
            sort1[y * 128 : y * 128 + 128] = packet_matrix(1, y)
            sort2[y * 128 : y * 128 + 128] = packet_matrix(2, y)

    weight = lifts[:, 0:128]
    for g in range(4):
        made = dot(thirds(f_ref[0, 8 * g : 8 * g + 8].reshape(256, 128)), weight)
        for k in range(8):
            x = 8 * g + k
            e = pltpu.roll(zz[0, x // 16], (124 - 8 * (x % 16)) % 128, 1)
            z1[pl.ds((x + 2) * 48 + 8, 32)] = made[32 * k : 32 * k + 32] - at_ends(e, 1)

    def cells(lev, x):
        step = STEPS[lev]
        return f_ref[0, x, pl.ds(0, 32 // step, stride=step), :]

    def ends_of(lev, part, k):
        step = STEPS[lev]
        n = 32 // step
        e = zz[0, part, pl.ds(0, n, stride=step), :] if step > 1 else zz[0, part]
        return at_ends(pick(e, end_index(n) + 8 * k), step)

    for lev, z, to in ((1, z2, lambda j: j * 32 + 8), (2, z3, lambda j: j * 24 + 8)):
        step = STEPS[lev]
        n = 32 // step
        v = jnp.concatenate([cells(lev, j * step) for j in range(n)], axis=0)
        made = dot(thirds(v), lifts[:, lev * 128 : lev * 128 + 128])
        for j in range(n):
            x = j * step
            z[pl.ds(to(j + 2), n)] = made[n * j : n * j + n] - ends_of(lev, x // 16, x % 16)

    def halo_cells(p, step):
        first, second, q = (other, core, p) if p < 4 else (core, other, p - 4)
        if step == 1:
            return jnp.where(odd == 1, first[0, q], second[0, q])
        some = pl.ds(0, 32 // step, stride=step)
        return jnp.where(odd == 1, first[0, q, some, :], second[0, q, some, :])

    for lev, (z, pitch) in enumerate(((z1, 48), (z2, 32), (z3, 24))):
        step = STEPS[lev]
        n = 32 // step
        which = ((0, n + 2), (1 + lev, n + 4), (6 - lev, 0))
        v = jnp.concatenate([halo_cells(p, step) for p, _ in which], axis=0)
        made = dot(thirds(v), lifts[:, lev * 128 : lev * 128 + 128])
        for k, (p, at) in enumerate(which):
            z[pl.ds(at * pitch + 8, n)] = made[n * k : n * k + n] - ends_of(lev, 2, p)

    made = dot(thirds(yy[0].reshape(TILES * 8, 128)), lifts[...])
    sub, index = subs(8), end_index(8)
    ends = []
    for t in range(TILES):
        if t < 16:
            e, chunk = yz[0, t // 8], jnp.where(sub < 5, 2 * t % 16, (2 * t + 1) % 16)
        elif t < 18:
            e, chunk = yz[0, 2 + t - 16], (sub // 2) * 4
        elif t == 18:
            e, chunk = yz[0, 4], 0
        else:
            e, chunk = yz[0, t - 14], jnp.where(sub < 3, t - 18, 25 - t)
        ends.append(pick(e, index + 8 * chunk))
    ends = jnp.concatenate(ends, axis=0)
    for lev, (z, pitch) in enumerate(((z1, 48), (z2, 32), (z3, 24))):
        step = STEPS[lev]
        n = 32 // step
        r = made[:, lev * 128 : lev * 128 + 128] - at_ends(ends, step)

        def put(j, first, second, last, z=z, pitch=pitch, n=n, r=r):
            for at, row in ((8 + n, first), (10 + n, second), (6, last)):
                z[pl.ds(j * pitch + at, 1)] = r[row : row + 1]

        for j in range(n):
            if lev == 0:
                at = (j // 2) * 8 + 5 * (j % 2)
                put(j + 2, at, at + 1, at + 2)
            elif lev == 1:
                put(j + 2, j * 8, j * 8 + 3, j * 8 + 4)
            else:
                put(j + 2, j * 16, 128 + 2 * j, 129 + 2 * j)
        put(n + 2, 18 * 8, 18 * 8 + 1 + lev, 18 * 8 + 6 - lev)
        at = (19 + lev) * 8
        put(n + 4, at, at + 1, at + 2)
        put(0, at + 3, at + 4, at + 5)

    def lift_plane(z, pitch, p):
        def plane(q):
            return z[pl.ds(pl.multiple_of(q * pitch, 8), pitch)]

        z[pl.ds(pl.multiple_of(p * pitch, 8), pitch)] = plane(p) - predicted(
            plane(p - 3), plane(p - 1), plane(p + 1), plane(p + 3)
        )

    def lift1(k, _):
        lift_plane(z1, 48, 2 * k + 3)
        return _

    lax.fori_loop(0, 16, lift1, 0, unroll=True)
    for k in range(8):
        lift_plane(z2, 32, 2 * k + 3)
    for k in range(4):
        lift_plane(z3, 24, 2 * k + 3)

    def lifted(load, count):
        low = [load(2 * j) for j in range(-1, count + 2)]
        high = [
            load(2 * j + 1) - predicted(low[j], low[j + 1], low[j + 2], low[j + 3])
            for j in range(count)
        ]
        return low[1 : count + 1], high

    parts = []
    for hx in range(2):
        sides = lifted(
            lambda y: z1[pl.ds((2 + hx) * 48 + 8 + y, 16, stride=96), :], 16
        )
        for side in sides:
            for top in range(2):
                tiles = [v.astype(BF16) for v in side[8 * top : 8 * top + 8]]
                parts.append(jnp.concatenate(tiles, axis=1))
    made = dot(jnp.concatenate(parts, axis=0), sort1[...])
    for c in range(8):
        for r in range(8):
            if c < 2 and r % 2 == 0:
                continue
            at = field * 1024 + ((c // 2) * 8 + r) * 32 + c % 2
            st1[pl.ds(at, 16, stride=2), :] = made[16 * c : 16 * c + 16, 128 * r : 128 * r + 128]

    even_lane = lanes(8) % 2 == 0
    parts = []
    for hx in range(2):
        sides = lifted(
            lambda y: z2[pl.ds((2 + hx) * 32 + 8 + y, 8, stride=64), :], 8
        )
        for side in sides:
            tiles = []
            for v in side:
                after = pltpu.roll(pltpu.roll(v, 7, 0), 1, 1)
                tiles.append(jnp.where(even_lane, v, after))
            parts.append(jnp.concatenate(tiles, axis=1))
    in2[pl.ds(pl.multiple_of(field * 32, 32), 32)] = jnp.concatenate(parts, axis=0).astype(BF16)

    lane8 = lanes(8)
    tiles = []
    for hx in range(2):
        acc = [None, None]
        for k in range(4):
            base = (2 * k + 2 + hx) * 24

            def rows_from(start, base=base):
                return z3[pl.ds(base + start, 4, stride=2), :]

            low = rows_from(8)
            high = rows_from(9) - predicted(rows_from(6), low, rows_from(10), rows_from(12))
            for hy, side in enumerate((low, high)):
                if k == 0:
                    acc[hy] = side
                else:
                    acc[hy] = jnp.where(lanes(4) % 4 == k, pltpu.roll(side, k, 1), acc[hy])
        t3[pl.ds(0, 4)] = acc[0]
        t3[pl.ds(4, 4)] = acc[1]
        tiles.append(shuffle(t3[pl.ds(0, 8)], shuffle_indices()))
    left = lane8 < 64
    a, c = tiles
    ar, cr = pltpu.roll(a, 64, 1), pltpu.roll(c, 64, 1)

    def above(t):
        return pltpu.roll(t, 1, 0)

    groups = (
        jnp.where(left, above(a), 0.0),
        jnp.where(left, a, above(a)),
        jnp.where(left, ar, above(cr)),
        jnp.where(left, c, above(c)),
        jnp.where(left, cr, 0.0),
    )
    for b in range(NB):
        for j, group in enumerate(groups):
            st3[pl.ds(field * 32 + b * 8 + j, 1)] = group[2 * b + 1 : 2 * b + 2]

    @pl.when(field == NF - 1)
    def _():
        made = dot(in2[...], sort2[...])
        for r in range(8):
            out2[r] = made[:, 128 * r : 128 * r + 128]
        total = lax.fori_loop(0, me[0], lambda i, s: s + cnt[i], jnp.int32(0))
        first = total % CAP

        def one(f, here):
            for b in range(NB):
                flags = [ret[(b * NF + f) * 3 + lev] for lev in range(3)]
                ring[pl.ds(here, 8)] = st3[pl.ds(pl.multiple_of(f * 32 + b * 8, 8), 8)]
                at2 = here + P0 + P3 * flags[2]
                at1 = at2 + P2 * flags[1]
                here = at1 + P1 * flags[0]

                @pl.when(flags[1] > 0)
                def _(b=b, at2=at2):
                    for s in range(1, 8):
                        r = b * 2 + s % 2
                        ring[pl.ds(at2 + (s - 1) * 4, 4)] = out2[
                            r, pl.ds(f * 32 + (s // 2) * 8, 4, stride=2), :
                        ]

                @pl.when(flags[0] > 0)
                def _(b=b, at1=at1):
                    for s in range(1, 8):
                        start = f * 1024 + ((s // 2) * 8 + b * 2 + s % 2) * 32
                        ring[pl.ds(at1 + (s - 1) * 32, 32)] = st1[
                            pl.ds(pl.multiple_of(start, 32), 32)
                        ]
            return here

        lax.fori_loop(0, NF, one, first)
        used = -(-CAP // rows)

        def fold(i, _):
            at = pl.multiple_of(i * rows, 8)
            near, far = ring[pl.ds(at, rows)], ring[pl.ds(at + CAP, rows)]
            out[i] = jnp.where(at + subs(rows) >= first, near, far).astype(BF16)
            return _

        lax.fori_loop(0, used, fold, 0, unroll=4)
        for block in range(used, nblk):
            out[block] = jnp.zeros((rows, 128), BF16)


def transform(me, counts, flags, fields, halos, blocks, rows):
    shapes = ((32, 32, 128),) + tuple(h.shape[1:] for h in halos)
    ring_rows = (2 * CAP + rows + 135) // 8 * 8
    return pl.pallas_call(
        main_kernel,
        grid=(NF,),
        in_specs=[smem(), smem(), smem()] + [field_block(*shape) for shape in shapes],
        out_specs=pl.BlockSpec((blocks, rows, 128), lambda f: (0, 0, 0)),
        out_shape=jax.ShapeDtypeStruct((blocks, rows, 128), BF16),
        scratch_shapes=[
            pltpu.VMEM((37 * 48, 128), F32),
            pltpu.VMEM((21 * 32, 128), F32),
            pltpu.VMEM((13 * 24, 128), F32),
            pltpu.VMEM((NF * 32, 1024), BF16),
            pltpu.VMEM((8, NF * 32, 128), F32),
            pltpu.VMEM((NF * 1024, 128), F32),
            pltpu.VMEM((NF * 32, 128), F32),
            pltpu.VMEM((32, 128), F32),
            pltpu.VMEM((ring_rows, 128), F32),
            pltpu.VMEM((384, 384), BF16),
            pltpu.VMEM((1024, 1024), BF16),
            pltpu.VMEM((1024, 1024), BF16),
        ],
        compiler_params=pltpu.CompilerParams(vmem_limit_bytes=48 * 2**20),
        name="transform",
    )(me, counts, flags, fields, *halos)


def route_kernel(me, cnt, recv, send):
    n, rows = recv.shape[0], recv.shape[1]
    slot = me[0] * rows + subs(rows)
    send[...] = jnp.zeros_like(send)

    def one(i, begin):
        count = cnt[i]
        place, first = begin // CAP, begin % CAP
        end = first + count
        value = recv[i]
        here = (slot >= first) & (slot < jnp.minimum(end, CAP))
        send[place] = jnp.where(here, value, send[place])

        @pl.when(end > CAP)
        def _():
            send[place + 1] = jnp.where(slot < end - CAP, value, send[place + 1])

        return begin + count

    lax.fori_loop(0, n, one, jnp.int32(0), unroll=4)


def route(me, counts, received):
    return pl.pallas_call(
        route_kernel,
        in_specs=[smem(), smem(), pl.BlockSpec(memory_space=pltpu.VMEM)],
        out_specs=pl.BlockSpec(memory_space=pltpu.VMEM),
        out_shape=jax.ShapeDtypeStruct(received.shape, BF16),
        compiler_params=pltpu.CompilerParams(vmem_limit_bytes=40 * 2**20),
        name="route",
    )(me, counts, received)


def swapped(value, n, axis, dy=0, dz=0):
    pairs = []
    for x in range(n):
        to = (x, x ^ 1, (x + 1 if x % 2 else x - 1) % n)[axis]
        for y in range(2):
            for z in range(2):
                there = (to * 2 + (y + dy) % 2) * 2 + (z + dz) % 2
                pairs.append(((x * 2 + y) * 2 + z, there))
    return lax.ppermute(value, ("gx", "gy", "gz"), pairs)


def per_device(n, fields, retained):
    me = lax.axis_index("gx").astype(jnp.int32).reshape(1)
    odd = me % 2
    flags = retained.reshape(-1)
    core, other = boundary_planes(odd, fields)
    core, other = swapped(core, n, 1), swapped(other, n, 2)
    yy, zz, yz, place = pack(me, flags, fields, core, other, n)
    counts = lax.psum(place, "gx")
    halos = (
        core,
        other,
        swapped(yy, n, 0, dy=1),
        swapped(zz, n, 0, dz=1),
        swapped(yz, n, 0, dy=1, dz=1),
    )
    rows = -(-CAP // (8 * n)) * 8
    ring = transform(me, counts, flags, fields, halos, n, rows)
    spread = lax.all_to_all(ring, "gx", 0, 0, tiled=True)
    routed = route(me, counts, spread)
    stream = lax.all_to_all(routed, "gx", 0, 0, tiled=True)
    return stream.reshape(1, 1, n * rows, 128)[:, :, :CAP]


def solution(mesh):
    placed = (P(None, "gx", "gy", "gz"), P("gx", "gy", "gz", None, None))
    return jax.shard_map(
        functools.partial(per_device, mesh.shape["gx"]),
        mesh=mesh,
        in_specs=placed,
        out_specs=P("gy", "gz", "gx", None),
        check_vma=False,
    )
```
